128 devices in a mesh: ctx: 16 (over x, y), head: 8 (over z, core).
Axes of the slice: x: 4, y: 4, z: 4, core: 2. Of those that a mesh axis runs over, the one named last changes fastest.
Arguments:
- head_inputs: bfloat16 [16384, 8192], P(('ctx', 'head')), may hold values from -6 to 6
- gate_inputs: bfloat16 [16384, 8192], P(('ctx', 'head')), may hold values from -6 to 6
- write_keys: bfloat16 [16384, 1024], P(('ctx', 'head')), may hold values from -6 to 6
- read_queries: bfloat16 [16384, 1024], P(('ctx', 'head')), may hold values from -0.5 to 0.5
- step_logits: bfloat16 [16384, 128], P(('ctx', 'head')), may hold values from -3 to 3
- step_bias: float32 [128], P('head'), may hold values from -6 to 0
- decay_log: float32 [128], P('head'), may hold values from -7 to -2
- skip_scale: float32 [128], P('head'), may hold values from 0.5 to 1.5
- norm_gain: float32 [8192], replicated, may hold values from 0.1 to 1.9
- document_starts: int32 [64], P('ctx'), may hold values from 0 to 256, as said below
Outputs:
- layer_output: bfloat16 [16384, 8192], P(('ctx', 'head'))
The draws below stay inside these ranges and needn't reach their ends.
Inputs may be any that keep to these rules, and one draw needn't show every extreme that they name: `document_starts`: each entry is the position within its block of 256 tokens at which a document starts, or 256 where none starts; the first block starts one at 0.
All inputs are finite; a program needn't handle non-finite values.
Results may differ from the reference program's by a relative error of at most 0.0058.
Values may be sent and summed in bfloat16 or wider, within the bound.
No kernel may reach another device: no remote copies, remote signals or barrier semaphores. Data moves between devices by JAX's collectives and lax.ppermute only.
A program may use at most 128 MiB of HBM per device.

```python
import jax
import jax.numpy as jnp
from jax import lax

HEADS = 128
HEAD_DIM = 64
STATE = 128
GROUPS = 8
BLOCK = 256
INNER = 8192
TOKENS = 16384


def decay_heads(key):
    rand_key = jax.random.fold_in(key, 11)
    spread = jax.random.uniform(rand_key, (HEADS,), jnp.float32)
    memory = 30.0 * (TOKENS / 30.0) ** spread
    step_size = 2.0 / jnp.sqrt(memory)
    return (memory, step_size)


def draw_step_bias(key, part):
    memory, step_size = decay_heads(key)
    return jnp.log(jnp.expm1(step_size)).astype(jnp.float32)


def draw_decay_log(key, part):
    memory, step_size = decay_heads(key)
    return (-jnp.log(memory * step_size)).astype(jnp.float32)


def draw_document_starts(key, part):
    count = TOKENS // BLOCK
    spacing = max(count // 4, 2)
    raw_draw = jax.random.randint(jax.random.fold_in(key, 5), (count,), 0, spacing * BLOCK)
    starts = jnp.where(raw_draw < BLOCK, raw_draw, BLOCK)
    return starts.at[0].set(0).astype(jnp.int32)


def steps_of(key, extent, pieces, smallest, largest):
    factor_of, own = 1.0, jax.random.fold_in(key, 6)
    for dim, shards_of in pieces:
        draws = jnp.exp(jax.random.uniform(jax.random.fold_in(own, dim), (shards_of,), jnp.float32, smallest / len(pieces), largest / len(pieces)))
        factor_of = factor_of * jnp.repeat(draws, extent[dim] // shards_of).reshape([-1 if axis == dim else 1 for axis in range(len(extent))])
    return factor_of


def gaussian(key, extent, width, most, pieces=(), kind=jnp.bfloat16):
    drawn = width * jax.random.normal(key, extent, jnp.float32)
    if pieces:
        drawn = drawn * steps_of(key, extent, pieces, -0.22, 0.18)
    return jnp.clip(drawn, -most, most).astype(kind)


def setup_inputs(seed: int = 0) -> dict:
    seeds = jax.random.split(jax.random.key(seed), 11)
    return {
        "head_inputs": gaussian(seeds[0], (TOKENS, INNER), 1.0, 6.0, ((0, 128),)),
        "gate_inputs": gaussian(seeds[1], (TOKENS, INNER), 1.0, 6.0, ((0, 128),)),
        "write_keys": gaussian(seeds[2], (TOKENS, GROUPS * STATE), 1.0, 6.0, ((0, 128),)),
        "read_queries": gaussian(seeds[3], (TOKENS, GROUPS * STATE), STATE ** -0.5, 0.5, ((0, 128),)),
        "step_logits": gaussian(seeds[4], (TOKENS, HEADS), 0.5, 3.0, ((0, 128),)),
        "step_bias": draw_step_bias(jax.random.fold_in(seeds[10], 71), 0),
        "decay_log": draw_decay_log(jax.random.fold_in(seeds[10], 71), 0),
        "skip_scale": jnp.clip(0.5 + 1.0 * jax.random.uniform(seeds[7], (HEADS,), jnp.float32) ** steps_of(seeds[7], (HEADS,), ((0, 8),), -0.2, 0.2), 0.5, 1.5),
        "norm_gain": jnp.clip(1.0 + 0.18 * jax.random.normal(seeds[8], (INNER,), jnp.float32), 0.1, 1.9),
        "document_starts": draw_document_starts(jax.random.fold_in(seeds[10], 71), 0),
    }


def block_terms(block_x, block_b, block_c, block_logit, start_at, step_bias, decay_log):
    length = block_x.shape[0]
    per_group = block_x.shape[1] // block_b.shape[1]
    step_size = jax.nn.softplus(block_logit.astype(jnp.float32) + step_bias)
    log_decay = -jnp.exp(decay_log) * step_size
    cumulative = jnp.cumsum(log_decay, axis=0)
    position = jnp.arange(length, dtype=jnp.int32)
    segment = position >= start_at
    allowed = (segment[:, None] == segment[None, :]) & (position[:, None] >= position[None, :])
    scores = jnp.einsum('tgn,sgn->gts', block_c.astype(jnp.float32), block_b.astype(jnp.float32))
    scores = jnp.repeat(scores, per_group, axis=0)
    across = cumulative.T
    spread = across[:, :, None] - across[:, None, :]
    damping = jnp.where(allowed[None], jnp.exp(jnp.where(allowed[None], spread, 0.0)), 0.0)
    mixing = lax.optimization_barrier((damping * scores * step_size.T[:, None, :]).astype(jnp.bfloat16))
    inside = jnp.einsum('hts,shp->thp', mixing.astype(jnp.float32), block_x.astype(jnp.float32))
    keep = segment == segment[length - 1]
    tail = jnp.where(keep[:, None], jnp.exp(cumulative[length - 1][None, :] - cumulative), 0.0) * step_size
    scaled = lax.optimization_barrier((block_x.astype(jnp.float32) * tail[:, :, None]).astype(jnp.bfloat16))
    keys_heads = jnp.repeat(block_b, per_group, axis=1)
    written = jnp.einsum('thp,thn->hpn', scaled.astype(jnp.float32), keys_heads.astype(jnp.float32))
    carried = jnp.where(start_at >= length, jnp.exp(cumulative[length - 1]), 0.0)
    return (inside, written, carried, cumulative, segment)

def reference(head_inputs, gate_inputs, write_keys, read_queries, step_logits, step_bias, decay_log, skip_scale, norm_gain, document_starts):
    blocks = TOKENS // BLOCK
    per_group = HEADS // GROUPS
    x_blocks = head_inputs.reshape(blocks, BLOCK, HEADS, HEAD_DIM)
    b_blocks = write_keys.reshape(blocks, BLOCK, GROUPS, STATE)
    c_blocks = read_queries.reshape(blocks, BLOCK, GROUPS, STATE)
    logit_blocks = step_logits.reshape(blocks, BLOCK, HEADS)

    def advance(carry_state, items):
        block_x, block_b, block_c, block_logit, start_at = items
        inside, written, carried, cumulative, segment = block_terms(block_x, block_b, block_c, block_logit, start_at, step_bias, decay_log)
        frozen = lax.optimization_barrier(carry_state.astype(jnp.bfloat16))
        query_heads = jnp.repeat(block_c, per_group, axis=1)
        outside = jnp.einsum('thn,hpn->thp', query_heads.astype(jnp.float32), frozen.astype(jnp.float32))
        factor = jnp.where(segment[:, None], 0.0, jnp.exp(cumulative))
        mixed = (inside + outside * factor[:, :, None] + skip_scale[None, :, None] * block_x.astype(jnp.float32)).astype(jnp.bfloat16)
        next_state = carried[:, None, None] * carry_state + written
        return (next_state, mixed)
    initial = jnp.zeros((HEADS, HEAD_DIM, STATE), jnp.float32)
    _, mixed = lax.scan(advance, initial, (x_blocks, b_blocks, c_blocks, logit_blocks, document_starts))
    scanned = mixed.reshape(TOKENS, HEADS * HEAD_DIM)
    gated = scanned.astype(jnp.float32) * jax.nn.silu(gate_inputs.astype(jnp.float32))
    power = lax.optimization_barrier(jnp.mean(gated * gated, axis=-1, keepdims=True))
    return (gated * lax.rsqrt(power + 1e-05) * norm_gain).astype(jnp.bfloat16)
```

```python
import functools

import jax
import jax.numpy as jnp
from jax import lax
from jax.experimental import pallas as pl
from jax.experimental.pallas import tpu as pltpu
from jax.sharding import PartitionSpec as P

HEADS = 128
HEAD_DIM = 64
STATE = 128
GROUPS = 8
BLOCK = 256
INNER = HEADS * HEAD_DIM
CHUNK = 128
PER_GROUP = HEADS // GROUPS
WIDE = PER_GROUP * HEAD_DIM
SLAB = 8
SLABS = STATE // SLAB
EPS = 1e-5

bf16 = jnp.bfloat16
f32 = jnp.float32


def iota(shape, axis):
    return lax.broadcasted_iota(jnp.int32, shape, axis)


def spreader(rows, parts):
    lane = iota((rows, WIDE), 0)
    head = iota((rows, WIDE), 1) // HEAD_DIM
    low = lane % 128
    hit = (low % PER_GROUP == head) & (low < parts * PER_GROUP)
    return jnp.where(hit, 1.0, 0.0).astype(bf16)


def to_front(v, group):
    return pltpu.roll(v, (HEADS - PER_GROUP * group) % HEADS, 1)


def spread(v, group, spread_ref):
    front = to_front(v, group)
    high = front.astype(bf16)
    low = (front - high.astype(f32)).astype(bf16)
    return jnp.dot(
        jnp.concatenate([high, low], axis=1), spread_ref[...], preferred_element_type=f32
    )


def softplus(v):
    return jnp.maximum(v, 0.0) + jnp.log1p(jnp.exp(-jnp.abs(v)))


def write_kernel(start_ref, logit_ref, bias_ref, decay_ref, x_ref, b_ref, pay_ref, p_ref, q_ref, spread_ref):
    group = pl.program_id(0)
    start = start_ref[0]

    @pl.when(group == 0)
    def _():
        step = softplus(logit_ref[...].astype(f32) + bias_ref[...])
        rate = -jnp.exp(decay_ref[...]) * step
        lower = jnp.where(iota((CHUNK, CHUNK), 0) >= iota((CHUNK, CHUNK), 1), 1.0, 0.0).astype(bf16)
        cum = jnp.zeros((CHUNK, HEADS), f32)
        rest = rate
        for _ in range(3):
            part = rest.astype(bf16)
            cum = cum + jnp.dot(lower, part, preferred_element_type=f32)
            rest = rest - part.astype(f32)
        p_ref[...] = jnp.exp(cum)
        q_ref[...] = jnp.exp(-cum) * step
        spread_ref[...] = spreader(2 * HEADS, 1)

    xq = (x_ref[...].astype(f32) * spread(q_ref[...], group, spread_ref)).astype(bf16)
    position = iota((CHUNK, STATE), 0)
    kept = (position >= start) | (start >= CHUNK)
    keys = jnp.where(kept, b_ref[...].astype(f32), 0.0).astype(bf16)
    written = lax.dot_general(keys, xq, (((0,), (0,)), ((), ())), preferred_element_type=f32)
    last = jnp.broadcast_to(p_ref[CHUNK - 1 : CHUNK, :], (SLAB, HEADS))
    written = written.reshape(SLABS, SLAB, WIDE) * spread(last, group, spread_ref)[None]
    pay_ref[:, 0, :, :WIDE] = written.astype(bf16)
    carried = to_front(jnp.where(start >= CHUNK, last, 0.0), group)
    high = carried.astype(bf16).astype(f32)
    middle = (carried - high).astype(bf16).astype(f32)
    low = carried - high - middle
    lane = iota((SLAB, HEADS), 1)
    packed = jnp.where(
        lane < PER_GROUP,
        high,
        jnp.where(
            lane < 2 * PER_GROUP,
            pltpu.roll(middle, PER_GROUP, 1),
            jnp.where(lane < 3 * PER_GROUP, pltpu.roll(low, 2 * PER_GROUP, 1), 0.0),
        ),
    ).astype(bf16)
    pay_ref[:, 0, :, WIDE:] = jnp.broadcast_to(packed[None], (SLABS, SLAB, HEADS))


def scan_kernel(chunks, pay_ref, out_ref, carried_ref):
    packed = pay_ref[:, :, WIDE:].astype(f32).reshape(chunks * SLAB, HEADS).astype(bf16)
    carried = jnp.dot(packed, spreader(HEADS, 3), preferred_element_type=f32)
    carried_ref[...] = carried.reshape(chunks, SLAB, WIDE)

    def one(k, state):
        out_ref[k] = state.astype(bf16)
        return carried_ref[k] * state + pay_ref[k, :, :WIDE].astype(f32)

    lax.fori_loop(0, chunks, one, jnp.zeros((SLAB, WIDE), f32), unroll=8)


def inside_kernel(start_ref, p_ref, q_ref, skip_ref, x_ref, b_ref, c_ref, y_ref, spread_ref):
    group = pl.program_id(0)
    start = start_ref[0]

    @pl.when(group == 0)
    def _():
        spread_ref[...] = spreader(2 * HEADS, 1)

    x = x_ref[...].astype(f32)
    xq = (x * spread(q_ref[...], group, spread_ref)).astype(bf16)
    score = lax.dot_general(c_ref[...], b_ref[...], (((1,), (1,)), ((), ())), preferred_element_type=f32)
    t = iota((CHUNK, CHUNK), 0)
    s = iota((CHUNK, CHUNK), 1)
    allowed = (s <= t) & ((t >= start) == (s >= start))
    mixing = jnp.where(allowed, score, 0.0).astype(bf16)
    inside = jnp.dot(mixing, xq, preferred_element_type=f32)
    skip = spread(jnp.broadcast_to(skip_ref[...], (SLAB, HEADS)), group, spread_ref)[:1]
    y_ref[...] = inside * spread(p_ref[...], group, spread_ref) + skip * x


def outside_kernel(start_ref, p_ref, y_ref, c_ref, state_ref, gate_ref, gain_ref, out_ref, gated_ref, power_ref, spread_ref):
    group = pl.program_id(0)
    start = start_ref[0]

    @pl.when(group == 0)
    def _():
        spread_ref[...] = spreader(2 * HEADS, 1)
        power_ref[...] = jnp.zeros_like(power_ref)

    seen = iota((CHUNK, STATE), 0) < start
    queries = jnp.where(seen, c_ref[...].astype(f32), 0.0).astype(bf16)
    state = state_ref[:, 0].astype(f32).reshape(STATE, WIDE).astype(bf16)
    outside = jnp.dot(queries, state, preferred_element_type=f32)
    mixed = y_ref[...] + outside * spread(p_ref[...], group, spread_ref)
    gate = gate_ref[...].astype(f32)
    gated = mixed * (gate / (1.0 + jnp.exp(-gate)))
    gated_ref[group] = gated
    power_ref[...] += jnp.sum(gated * gated, axis=1, keepdims=True)

    @pl.when(group == GROUPS - 1)
    def _():
        scale = lax.rsqrt(power_ref[...] * (1.0 / INNER) + EPS)
        for g in range(GROUPS):
            columns = slice(g * WIDE, (g + 1) * WIDE)
            out_ref[:, columns] = (gated_ref[g] * scale * gain_ref[:, columns]).astype(bf16)


def params(mib):
    return pltpu.CompilerParams(
        dimension_semantics=("arbitrary",), vmem_limit_bytes=mib * 2**20
    )


def local(
    head_inputs,
    gate_inputs,
    write_keys,
    read_queries,
    step_logits,
    step_bias,
    decay_log,
    skip_scale,
    norm_gain,
    document_starts,
):
    half = lax.axis_index("head") % 2
    block_start = document_starts[lax.axis_index("head") // 2]
    begun = block_start - half * CHUNK
    start = jnp.where((begun >= 0) & (begun < CHUNK), begun, CHUNK).reshape(1)
    own = jnp.stack([step_bias, decay_log, skip_scale])
    heads = lax.all_gather(own, "head", axis=1, tiled=True)
    bias, decay, skip = heads[0:1], heads[1:2], heads[2:3]

    smem = pl.BlockSpec(memory_space=pltpu.SMEM)
    small = pl.BlockSpec((CHUNK, HEADS), lambda g: (0, 0))
    row = pl.BlockSpec((1, HEADS), lambda g: (0, 0))
    channels = pl.BlockSpec((CHUNK, WIDE), lambda g: (0, g))
    states = pl.BlockSpec((CHUNK, STATE), lambda g: (0, g))
    table = jax.ShapeDtypeStruct((CHUNK, HEADS), f32)
    spread_scratch = pltpu.VMEM((2 * HEADS, WIDE), bf16)
    chunks = SLABS * GROUPS

    pay, p, q = pl.pallas_call(
        write_kernel,
        grid=(GROUPS,),
        in_specs=[smem, small, row, row, channels, states],
        out_specs=[
            pl.BlockSpec((SLABS, 1, SLAB, WIDE + HEADS), lambda g: (0, g, 0, 0)),
            small,
            small,
        ],
        out_shape=[
            jax.ShapeDtypeStruct((SLABS, GROUPS, SLAB, WIDE + HEADS), bf16),
            table,
            table,
        ],
        scratch_shapes=[spread_scratch],
        compiler_params=params(32),
        cost_estimate=pl.CostEstimate(flops=2 * 2 * CHUNK * STATE * INNER, bytes_accessed=5 * 2**20, transcendentals=0),
        name="write",
    )(start, step_logits, bias, decay, head_inputs, write_keys)

    arrived = lax.all_to_all(
        pay.reshape(chunks, SLAB, WIDE + HEADS), ("ctx", "head"), 0, 0, tiled=True
    )

    y = pl.pallas_call(
        inside_kernel,
        grid=(GROUPS,),
        in_specs=[smem, small, small, row, channels, states, states],
        out_specs=channels,
        out_shape=jax.ShapeDtypeStruct((CHUNK, INNER), f32),
        scratch_shapes=[spread_scratch],
        compiler_params=params(32),
        cost_estimate=pl.CostEstimate(flops=2 * 4 * CHUNK * STATE * INNER, bytes_accessed=7 * 2**20, transcendentals=0),
        name="inside",
    )(start, p, q, skip, head_inputs, write_keys, read_queries)

    frozen = pl.pallas_call(
        functools.partial(scan_kernel, chunks),
        out_shape=jax.ShapeDtypeStruct((chunks, SLAB, WIDE), bf16),
        scratch_shapes=[pltpu.VMEM((chunks, SLAB, WIDE), f32)],
        compiler_params=pltpu.CompilerParams(vmem_limit_bytes=32 * 2**20),
        name="scan",
    )(arrived)

    returned = lax.all_to_all(frozen, ("ctx", "head"), 0, 0, tiled=True)

    return pl.pallas_call(
        outside_kernel,
        grid=(GROUPS,),
        in_specs=[
            smem,
            small,
            channels,
            states,
            pl.BlockSpec((SLABS, 1, SLAB, WIDE), lambda g: (0, g, 0, 0)),
            channels,
            pl.BlockSpec((1, INNER), lambda g: (0, 0)),
        ],
        out_specs=pl.BlockSpec((CHUNK, INNER), lambda g: (0, 0)),
        out_shape=jax.ShapeDtypeStruct((CHUNK, INNER), bf16),
        scratch_shapes=[
            pltpu.VMEM((GROUPS, CHUNK, WIDE), f32),
            pltpu.VMEM((CHUNK, 1), f32),
            spread_scratch,
        ],
        compiler_params=params(32),
        name="outside",
    )(
        start,
        p,
        y,
        read_queries,
        returned.reshape(SLABS, GROUPS, SLAB, WIDE),
        gate_inputs,
        norm_gain.reshape(1, INNER),
    )


def solution(mesh):
    tokens = P(("ctx", "head"), None)
    return jax.shard_map(
        local,
        mesh=mesh,
        in_specs=(tokens,) * 5 + (P("head"),) * 3 + (P(), P("ctx")),
        out_specs=tokens,
        check_vma=False,
    )
```

```python
import functools

import jax
import jax.numpy as jnp
from jax import lax
from jax.experimental import pallas as pl
from jax.experimental.pallas import tpu as pltpu
from jax.sharding import Mesh
from jax.sharding import PartitionSpec as P

HEADS = 128
HEAD_DIM = 64
STATE = 128
GROUPS = 8
INNER = HEADS * HEAD_DIM
CHUNK = 128
CORES = 2
HALF = GROUPS // CORES
HALF_HEADS = HEADS // CORES
PER_GROUP = HEADS // GROUPS
WIDE = PER_GROUP * HEAD_DIM
HALF_WIDE = HALF * WIDE
SLAB = 8
SLABS = STATE // SLAB
LANES = 128
EPS = 1e-5

bf16 = jnp.bfloat16
f32 = jnp.float32


def iota(shape, axis):
    return lax.broadcasted_iota(jnp.int32, shape, axis)


def spreader(rows, parts):
    lane = iota((rows, WIDE), 0) % LANES
    head = iota((rows, WIDE), 1) // HEAD_DIM
    hit = (lane % PER_GROUP == head) & (lane < parts * PER_GROUP)
    return jnp.where(hit, 1.0, 0.0).astype(bf16)


def to_front(v, group):
    return pltpu.roll(v, (LANES - PER_GROUP * group) % LANES, 1)


def spread(v, group, spread_ref):
    front = to_front(v, group)
    high = front.astype(bf16)
    low = (front - high.astype(f32)).astype(bf16)
    return jnp.dot(
        jnp.concatenate([high, low], axis=1), spread_ref[...], preferred_element_type=f32
    )


def softplus(v):
    return jnp.maximum(v, 0.0) + jnp.log1p(jnp.exp(-jnp.abs(v)))


def cumulated(step, decay):
    rate = -jnp.exp(decay) * step
    lower = jnp.where(iota((CHUNK, CHUNK), 0) >= iota((CHUNK, CHUNK), 1), 1.0, 0.0).astype(bf16)
    cum = jnp.zeros(rate.shape, f32)
    for _ in range(3):
        part = rate.astype(bf16)
        cum = cum + jnp.dot(lower, part, preferred_element_type=f32)
        rate = rate - part.astype(f32)
    return jnp.exp(cum), jnp.exp(-cum) * step


def chunk_start(place, starts_ref, core):
    begun = starts_ref[place // CORES] - core * CHUNK
    return jnp.where((begun >= 0) & (begun < CHUNK), begun, CHUNK)


def write_kernel(
    place_ref, starts_ref, *refs
):
    own_refs, (logit_ref, logit_got_ref, x_ref, x_got_ref, b_ref, b_got_ref) = refs[:HALF], refs[HALF : HALF + 6]
    pay_ref, middle_ref, params_ref, decay_ref, p_ref, q_ref, spread_ref = refs[HALF + 6 :]
    group = pl.program_id(0)
    place = place_ref[0]
    core = place % CORES

    @pl.when(group == 0)
    def _():
        spread_ref[...] = spreader(2 * LANES, 1)
        lane = iota((SLAB, LANES), 1)
        params = jnp.zeros((SLAB, LANES), f32)
        for turn in range(HALF):
            some = jnp.where(lane < PER_GROUP, own_refs[turn][...], 0.0)
            params = params + pltpu.roll(some, PER_GROUP * ((place // CORES + turn) % HALF), 1)
        params_ref[...] = params
        half = iota((CHUNK, LANES), 1) < HALF_HEADS
        for chunk, ref in enumerate((logit_ref, logit_got_ref)):
            logit = pltpu.roll(ref[...].astype(f32), (LANES - HALF_HEADS * core) % LANES, 1)
            step = jnp.where(half, softplus(logit + params[0:1]), 0.0)
            p_ref[chunk], q_ref[chunk] = cumulated(step, params[1:2])

    def states(chunk, of_core, x, b):
        start = chunk_start(place, starts_ref, of_core)
        xq = (x[...].astype(f32) * spread(q_ref[chunk], group, spread_ref)).astype(bf16)
        kept = (iota((CHUNK, STATE), 0) >= start) | (start >= CHUNK)
        keys = jnp.where(kept, b[...].astype(f32), 0.0).astype(bf16)
        written = lax.dot_general(keys, xq, (((0,), (0,)), ((), ())), preferred_element_type=f32)
        last = jnp.broadcast_to(p_ref[chunk, CHUNK - 1 : CHUNK, :], (SLAB, LANES))
        wide = spread(last, group, spread_ref)
        written = written.reshape(SLABS, SLAB, WIDE) * wide[None]
        return written, jnp.where(start >= CHUNK, last, 0.0), jnp.where(start >= CHUNK, wide, 0.0)

    def body(first, second):
        before, decay_before, _ = states(*first)
        after, decay_after, wide_after = states(*second)
        middle_ref[...] = before.reshape(STATE, WIDE)
        decay_ref[...] = decay_before
        pay_ref[:, 0, :, :WIDE] = (before * wide_after[None] + after).astype(bf16)
        carried = to_front(decay_before * decay_after, group)
        high = carried.astype(bf16).astype(f32)
        middle = (carried - high).astype(bf16).astype(f32)
        low = carried - high - middle
        lane = iota((SLAB, LANES), 1)
        packed = jnp.where(
            lane < PER_GROUP,
            high,
            jnp.where(
                lane < 2 * PER_GROUP,
                pltpu.roll(middle, PER_GROUP, 1),
                jnp.where(lane < 3 * PER_GROUP, pltpu.roll(low, 2 * PER_GROUP, 1), 0.0),
            ),
        ).astype(bf16)
        pay_ref[:, 0, :, WIDE:] = jnp.broadcast_to(packed[None], (SLABS, SLAB, LANES))

    mine = (0, core, x_ref, b_ref)
    other = (1, 1 - core, x_got_ref, b_got_ref)

    @pl.when(core == 0)
    def _():
        body(mine, other)

    @pl.when(core == 1)
    def _():
        body(other, mine)


def scan_kernel(blocks, pay_ref, out_ref, carried_ref):
    packed = pay_ref[:, :, WIDE:].astype(f32).reshape(blocks * SLAB, LANES).astype(bf16)
    carried = jnp.dot(packed, spreader(LANES, 3), preferred_element_type=f32)
    carried_ref[...] = carried.reshape(blocks, SLAB, WIDE)

    def one(k, state):
        out_ref[k] = state.astype(bf16)
        return carried_ref[k] * state + pay_ref[k, :, :WIDE].astype(f32)

    lax.fori_loop(0, blocks, one, jnp.zeros((SLAB, WIDE), f32), unroll=8)


def inside_kernel(
    place_ref, starts_ref, params_ref, got_ref, logit_ref, x_ref, b_ref, c_ref, gate_ref,
    base_ref, factor_ref, p_ref, q_ref, skip_ref, spread_ref,
):
    group = pl.program_id(0)
    place = place_ref[0]
    core = place % CORES
    start = chunk_start(place, starts_ref, core)

    @pl.when(group == 0)
    def _():
        spread_ref[...] = spreader(2 * LANES, 1)
        params = pltpu.roll(params_ref[...], HALF_HEADS * core, 1) + pltpu.roll(
            got_ref[...], HALF_HEADS * (1 - core), 1
        )
        skip_ref[...] = jnp.broadcast_to(params[2:3], (SLAB, LANES))
        step = softplus(logit_ref[...].astype(f32) + params[0:1])
        p_ref[...], q_ref[...] = cumulated(step, params[1:2])

    x = x_ref[...].astype(f32)
    xq = (x * spread(q_ref[...], group, spread_ref)).astype(bf16)
    score = lax.dot_general(c_ref[...], b_ref[...], (((1,), (1,)), ((), ())), preferred_element_type=f32)
    t = iota((CHUNK, CHUNK), 0)
    s = iota((CHUNK, CHUNK), 1)
    allowed = (s <= t) & ((t >= start) == (s >= start))
    mixing = jnp.where(allowed, score, 0.0).astype(bf16)
    inside = jnp.dot(mixing, xq, preferred_element_type=f32)
    skip = spread(skip_ref[...], group, spread_ref)[:1]
    gate = gate_ref[...].astype(f32)
    silu = gate / (1.0 + jnp.exp(-gate))
    grown = spread(p_ref[...], group, spread_ref)
    base_ref[...] = ((inside * grown + skip * x) * silu).astype(bf16)
    factor_ref[...] = (grown * silu).astype(bf16)


def states_kernel(place_ref, starts_ref, state_ref, middle_ref, decay_ref, own_ref, sent_ref, spread_ref):
    group = pl.program_id(0)
    core = place_ref[0] % CORES

    @pl.when(group == 0)
    def _():
        spread_ref[...] = spreader(2 * LANES, 1)

    block = state_ref[:, 0].astype(f32)
    decay = spread(decay_ref[...], group, spread_ref)
    first = block.reshape(STATE, WIDE).astype(bf16)
    second = ((block * decay[None]).reshape(STATE, WIDE) + middle_ref[...]).astype(bf16)

    @pl.when(core == 0)
    def _():
        own_ref[...] = first
        sent_ref[...] = second

    @pl.when(core == 1)
    def _():
        own_ref[...] = second
        sent_ref[...] = first


def gated_part(place_ref, starts_ref, base_ref, factor_ref, c_ref, state_ref):
    place = place_ref[0]
    start = chunk_start(place, starts_ref, place % CORES)
    seen = iota((CHUNK, STATE), 0) < start
    queries = jnp.where(seen, c_ref[...].astype(f32), 0.0).astype(bf16)
    outside = jnp.dot(queries, state_ref[...], preferred_element_type=f32)
    gated = base_ref[...].astype(f32) + outside * factor_ref[...].astype(f32)
    squares = gated * gated
    power = squares[:, :LANES]
    for i in range(1, WIDE // LANES):
        power = power + squares[:, i * LANES : (i + 1) * LANES]
    return gated, power


def own_kernel(place_ref, starts_ref, base_ref, factor_ref, c_ref, state_ref, gated_ref, power_ref):
    gated, power = gated_part(place_ref, starts_ref, base_ref, factor_ref, c_ref, state_ref)
    gated_ref[...] = gated

    @pl.when(pl.program_id(0) == 0)
    def _():
        power_ref[...] = jnp.zeros_like(power_ref)

    power_ref[...] += power


def last_kernel(
    place_ref, starts_ref, base_ref, factor_ref, c_ref, state_ref, gated_own_ref, power_own_ref, gain_ref, out_ref, gated_ref, power_ref
):
    group = pl.program_id(0)
    gated, power = gated_part(place_ref, starts_ref, base_ref, factor_ref, c_ref, state_ref)
    gated_ref[group] = gated

    @pl.when(group == 0)
    def _():
        power_ref[...] = power_own_ref[...]

    power_ref[...] += power

    @pl.when(group == HALF - 1)
    def _():
        total = jnp.sum(power_ref[...], axis=1, keepdims=True)
        scale = lax.rsqrt(total * (1.0 / INNER) + EPS)
        core = place_ref[0] % CORES
        for g in range(HALF):
            own = pl.ds(pl.multiple_of(core * HALF_WIDE + g * WIDE, WIDE), WIDE)
            out_ref[:, own] = (gated_own_ref[:, g * WIDE : (g + 1) * WIDE] * scale * gain_ref[:, own]).astype(bf16)
            other = pl.ds(pl.multiple_of((1 - core) * HALF_WIDE + g * WIDE, WIDE), WIDE)
            out_ref[:, other] = (gated_ref[g] * scale * gain_ref[:, other]).astype(bf16)


def local(
    head_inputs,
    gate_inputs,
    write_keys,
    read_queries,
    step_logits,
    step_bias,
    decay_log,
    skip_scale,
    norm_gain,
    document_starts,
):
    depth = lax.axis_size("z")
    blocks = lax.axis_size("ctx") * depth
    core = lax.axis_index("core")
    place = (lax.axis_index("z") * CORES + core).astype(jnp.int32).reshape(1)
    swap = [(0, 1), (1, 0)]
    devices = depth * CORES

    own = jnp.pad(jnp.stack([step_bias, decay_log, skip_scale]), ((0, SLAB - 3), (0, LANES - PER_GROUP)))
    turns = [
        lax.ppermute(
            own,
            ("z", "core"),
            [(HALF * (i % CORES) + (i // CORES + turn) % HALF, i) for i in range(devices)],
        )
        for turn in range(HALF)
    ]
    x_got = lax.ppermute(
        lax.dynamic_slice(head_inputs, (0, (1 - core) * HALF_WIDE), (CHUNK, HALF_WIDE)), "core", swap
    )
    b_got = lax.ppermute(
        lax.dynamic_slice(write_keys, (0, (1 - core) * HALF * STATE), (CHUNK, HALF * STATE)), "core", swap
    )
    logit_got = lax.ppermute(step_logits, "core", swap)

    def call(kernel, steps, ins, outs, out_shape, scratch, name, cost=None):
        return pl.pallas_call(
            kernel,
            grid_spec=pltpu.PrefetchScalarGridSpec(
                num_scalar_prefetch=2,
                grid=(steps,),
                in_specs=ins,
                out_specs=outs,
                scratch_shapes=scratch,
            ),
            out_shape=out_shape,
            compiler_params=pltpu.CompilerParams(
                dimension_semantics=("arbitrary",), vmem_limit_bytes=56 * 2**20
            ),
            cost_estimate=cost,
            name=name,
        )

    def shape(dims, kind):
        return jax.ShapeDtypeStruct(dims, kind)

    def fixed(*dims):
        return pl.BlockSpec(dims, lambda g, place, starts: (0,) * len(dims))

    def plain(width):
        return pl.BlockSpec((CHUNK, width), lambda g, place, starts: (0, g))

    def mine(width):
        return pl.BlockSpec((CHUNK, width), lambda g, place, starts: (0, HALF * (place[0] % CORES) + g))

    def others(width):
        return pl.BlockSpec((CHUNK, width), lambda g, place, starts: (0, HALF * (1 - place[0] % CORES) + g))

    def slabs(width):
        return pl.BlockSpec((SLABS, 1, SLAB, width), lambda g, place, starts: (0, g, 0, 0))

    small = fixed(CHUNK, LANES)
    row = fixed(SLAB, LANES)
    spread_scratch = pltpu.VMEM((2 * LANES, WIDE), bf16)
    table = pltpu.VMEM((CHUNK, LANES), f32)
    tables = pltpu.VMEM((2, CHUNK, LANES), f32)

    pay, middle, params, decay = call(
        write_kernel,
        HALF,
        [row] * HALF + [small, small, mine(WIDE), plain(WIDE), mine(STATE), plain(STATE)],
        [slabs(WIDE + LANES), plain(WIDE), row, row],
        [
            shape((SLABS, HALF, SLAB, WIDE + LANES), bf16),
            shape((STATE, HALF_WIDE), f32),
            shape((SLAB, LANES), f32),
            shape((SLAB, LANES), f32),
        ],
        [tables, tables, spread_scratch],
        "write",
    )(place, document_starts, *turns, step_logits, logit_got, head_inputs, x_got, write_keys, b_got)

    arrived = lax.all_to_all(
        pay.reshape(blocks, SLAB, WIDE + LANES), ("ctx", "z"), 0, 0, tiled=True
    )
    params_got = lax.ppermute(params, "core", swap)

    base, factor = call(
        inside_kernel,
        GROUPS,
        [row, row, small, plain(WIDE), plain(STATE), plain(STATE), plain(WIDE)],
        [plain(WIDE), plain(WIDE)],
        [shape((CHUNK, INNER), bf16), shape((CHUNK, INNER), bf16)],
        [table, table, pltpu.VMEM((SLAB, LANES), f32), spread_scratch],
        "inside",
        pl.CostEstimate(flops=2 * 4 * CHUNK * STATE * INNER, bytes_accessed=9 * 2**20, transcendentals=2**20),
    )(place, document_starts, params, params_got, step_logits, head_inputs, write_keys, read_queries, gate_inputs)

    frozen = pl.pallas_call(
        functools.partial(scan_kernel, blocks),
        out_shape=shape((blocks, SLAB, WIDE), bf16),
        scratch_shapes=[pltpu.VMEM((blocks, SLAB, WIDE), f32)],
        compiler_params=pltpu.CompilerParams(vmem_limit_bytes=32 * 2**20),
        name="scan",
    )(arrived)

    returned = lax.all_to_all(frozen, ("ctx", "z"), 0, 0, tiled=True)

    half_state = shape((STATE, HALF_WIDE), bf16)
    state_own, state_sent = call(
        states_kernel,
        HALF,
        [slabs(WIDE), plain(WIDE), row],
        [plain(WIDE), plain(WIDE)],
        [half_state, half_state],
        [spread_scratch],
        "states",
    )(place, document_starts, returned.reshape(SLABS, HALF, SLAB, WIDE), middle, decay)

    state_got = lax.ppermute(state_sent, "core", swap)

    gated, power = call(
        own_kernel,
        HALF,
        [mine(WIDE), mine(WIDE), mine(STATE), plain(WIDE)],
        [plain(WIDE), small],
        [shape((CHUNK, HALF_WIDE), f32), shape((CHUNK, LANES), f32)],
        [],
        "own",
        pl.CostEstimate(flops=2 * CHUNK * STATE * INNER, bytes_accessed=5 * 2**20, transcendentals=0),
    )(place, document_starts, base, factor, read_queries, state_own)

    return call(
        last_kernel,
        HALF,
        [
            others(WIDE),
            others(WIDE),
            others(STATE),
            plain(WIDE),
            fixed(CHUNK, HALF_WIDE),
            small,
            fixed(1, INNER),
        ],
        fixed(CHUNK, INNER),
        shape((CHUNK, INNER), bf16),
        [pltpu.VMEM((HALF, CHUNK, WIDE), f32), table],
        "last",
    )(place, document_starts, base, factor, read_queries, state_got, gated, power, norm_gain.reshape(1, INNER))


def solution(mesh):
    ctx, head = mesh.devices.shape
    split = Mesh(mesh.devices.reshape(ctx, head // CORES, CORES), ("ctx", "z", "core"))
    tokens = P(("ctx", "z", "core"), None)
    return jax.shard_map(
        local,
        mesh=split,
        in_specs=(tokens,) * 5 + (P(("z", "core")),) * 3 + (P(), P("ctx")),
        out_specs=tokens,
        check_vma=False,
    )
```

```python
import functools

import jax
import jax.numpy as jnp
from jax import lax
from jax.experimental import pallas as pl
from jax.experimental.pallas import tpu as pltpu
from jax.sharding import Mesh
from jax.sharding import PartitionSpec as P

HEADS = 128
HEAD_DIM = 64
STATE = 128
GROUPS = 8
INNER = HEADS * HEAD_DIM
CHUNK = 128
CORES = 2
HALF = GROUPS // CORES
HALF_HEADS = HEADS // CORES
PER_GROUP = HEADS // GROUPS
WIDE = PER_GROUP * HEAD_DIM
HALF_WIDE = HALF * WIDE
SLAB = 8
SLABS = STATE // SLAB
LANES = 128
PARTS = 4
EPS = 1e-5

bf16 = jnp.bfloat16
f32 = jnp.float32


def iota(shape, axis):
    return lax.broadcasted_iota(jnp.int32, shape, axis)


def spreader(rows, parts):
    lane = iota((rows, WIDE), 0) % LANES
    head = iota((rows, WIDE), 1) // HEAD_DIM
    hit = (lane % PER_GROUP == head) & (lane < parts * PER_GROUP)
    return jnp.where(hit, 1.0, 0.0).astype(bf16)


def to_front(v, group):
    return pltpu.roll(v, (LANES - PER_GROUP * group) % LANES, 1)


def spread(v, group, spread_ref):
    front = to_front(v, group)
    high = front.astype(bf16)
    low = (front - high.astype(f32)).astype(bf16)
    return jnp.dot(
        jnp.concatenate([high, low], axis=1), spread_ref[...], preferred_element_type=f32
    )


def softplus(v):
    return jnp.maximum(v, 0.0) + jnp.log1p(jnp.exp(-jnp.abs(v)))


def cumulated(step, decay):
    rate = -jnp.exp(decay) * step
    lower = jnp.where(iota((CHUNK, CHUNK), 0) >= iota((CHUNK, CHUNK), 1), 1.0, 0.0).astype(bf16)
    cum = jnp.zeros(rate.shape, f32)
    for _ in range(3):
        part = rate.astype(bf16)
        cum = cum + jnp.dot(lower, part, preferred_element_type=f32)
        rate = rate - part.astype(f32)
    return jnp.exp(cum), jnp.exp(-cum) * step


def chunk_start(place, starts_ref, core):
    begun = starts_ref[place // CORES] - core * CHUNK
    return jnp.where((begun >= 0) & (begun < CHUNK), begun, CHUNK)


def write_kernel(
    place_ref, starts_ref, own0, own1, own2, own3, logit_ref, logit_got_ref, x_ref, x_got_ref, b_ref, b_got_ref,
    pay_ref, middle_ref, params_ref, decay_ref, spread_ref,
):
    place = place_ref[0]
    core = place % CORES
    spread_ref[...] = spreader(2 * LANES, 1)
    lane = iota((SLAB, LANES), 1)
    params = jnp.zeros((SLAB, LANES), f32)
    for turn, ref in enumerate((own0, own1, own2, own3)):
        some = jnp.where(lane < PER_GROUP, ref[...], 0.0)
        params = params + pltpu.roll(some, PER_GROUP * ((place // CORES + turn) % HALF), 1)
    params_ref[...] = params
    half = iota((CHUNK, LANES), 1) < HALF_HEADS
    chunks = []
    for ref, of_core in ((logit_ref, core), (logit_got_ref, 1 - core)):
        logit = pltpu.roll(ref[...].astype(f32), (LANES - HALF_HEADS * core) % LANES, 1)
        step = jnp.where(half, softplus(logit + params[0:1]), 0.0)
        p, q = cumulated(step, params[1:2])
        start = chunk_start(place, starts_ref, of_core)
        last = jnp.broadcast_to(p[CHUNK - 1 : CHUNK, :], (SLAB, LANES))
        kept = (iota((CHUNK, STATE), 0) >= start) | (start >= CHUNK)
        chunks.append((q, last, jnp.where(start >= CHUNK, last, 0.0), kept))
    whole = chunks[0][2] * chunks[1][2]
    high = whole.astype(bf16).astype(f32)
    middle = (whole - high).astype(bf16).astype(f32)
    low = whole - high - middle
    first_decay = jnp.where(core == 0, chunks[0][2], chunks[1][2])
    second_decay = jnp.where(core == 0, chunks[1][2], chunks[0][2])
    decay_ref[...] = first_decay

    for group in range(HALF):
        at = group * WIDE
        own_at = pl.multiple_of(core * HALF_WIDE + at, WIDE)
        own_key = pl.multiple_of((core * HALF + group) * STATE, STATE)
        xs = (x_ref[:, pl.ds(own_at, WIDE)], x_got_ref[:, at : at + WIDE])
        keys = (b_ref[:, pl.ds(own_key, STATE)], b_got_ref[:, group * STATE : (group + 1) * STATE])
        written = []
        for (q, last, _, kept), x, b in zip(chunks, xs, keys):
            xq = (x.astype(f32) * spread(q, group, spread_ref)).astype(bf16)
            b = jnp.where(kept, b.astype(f32), 0.0).astype(bf16)
            w = lax.dot_general(b, xq, (((0,), (0,)), ((), ())), preferred_element_type=f32)
            written.append(w.reshape(SLABS, SLAB, WIDE) * spread(last, group, spread_ref)[None])
        before = jnp.where(core == 0, written[0], written[1])
        after = jnp.where(core == 0, written[1], written[0])
        middle_ref[:, at : at + WIDE] = before.reshape(STATE, WIDE)
        pay_ref[:, group, :, :WIDE] = (before * spread(second_decay, group, spread_ref)[None] + after).astype(bf16)
        packed = jnp.where(
            lane < PER_GROUP,
            to_front(high, group),
            jnp.where(
                lane < 2 * PER_GROUP,
                to_front(middle, group - 1),
                jnp.where(lane < 3 * PER_GROUP, to_front(low, group - 2), 0.0),
            ),
        ).astype(bf16)
        pay_ref[:, group, :, WIDE:] = jnp.broadcast_to(packed[None], (SLABS, SLAB, LANES))


def scan_kernel(blocks, pay_ref, out_ref, carried_ref):
    packed = pay_ref[:, :, WIDE:].astype(f32).reshape(blocks * SLAB, LANES).astype(bf16)
    carried = jnp.dot(packed, spreader(LANES, 3), preferred_element_type=f32)
    carried_ref[...] = carried.reshape(blocks, SLAB, WIDE)

    def one(k, state):
        out_ref[k] = state.astype(bf16)
        return carried_ref[k] * state + pay_ref[k, :, :WIDE].astype(f32)

    lax.fori_loop(0, blocks, one, jnp.zeros((SLAB, WIDE), f32), unroll=8)


def inside_kernel(
    place_ref, starts_ref, params_ref, got_ref, logit_ref, x_ref, b_ref, c_ref, gate_ref,
    base_ref, factor_ref, spread_ref,
):
    place = place_ref[0]
    core = place % CORES
    start = chunk_start(place, starts_ref, core)
    spread_ref[...] = spreader(2 * LANES, 1)
    params = pltpu.roll(params_ref[...], HALF_HEADS * core, 1) + pltpu.roll(
        got_ref[...], HALF_HEADS * (1 - core), 1
    )
    skips = jnp.broadcast_to(params[2:3], (SLAB, LANES))
    step = softplus(logit_ref[...].astype(f32) + params[0:1])
    p, q = cumulated(step, params[1:2])
    t = iota((CHUNK, CHUNK), 0)
    s = iota((CHUNK, CHUNK), 1)
    allowed = (s <= t) & ((t >= start) == (s >= start))
    for group in range(GROUPS):
        columns = slice(group * WIDE, (group + 1) * WIDE)
        states = slice(group * STATE, (group + 1) * STATE)
        x = x_ref[:, columns].astype(f32)
        xq = (x * spread(q, group, spread_ref)).astype(bf16)
        score = lax.dot_general(
            c_ref[:, states], b_ref[:, states], (((1,), (1,)), ((), ())), preferred_element_type=f32
        )
        mixing = jnp.where(allowed, score, 0.0).astype(bf16)
        inside = jnp.dot(mixing, xq, preferred_element_type=f32)
        skip = spread(skips, group, spread_ref)[:1]
        gate = gate_ref[:, columns].astype(f32)
        silu = gate / (1.0 + jnp.exp(-gate))
        grown = spread(p, group, spread_ref)
        base_ref[:, columns] = ((inside * grown + skip * x) * silu).astype(bf16)
        factor_ref[:, columns] = (grown * silu).astype(bf16)


def states_kernel(place_ref, state_ref, middle_ref, decay_ref, own_ref, sent_ref, spread_ref):
    core = place_ref[0] % CORES
    spread_ref[...] = spreader(2 * LANES, 1)
    for group in range(HALF):
        columns = slice(group * WIDE, (group + 1) * WIDE)
        block = state_ref[:, group].astype(f32)
        decay = spread(decay_ref[...], group, spread_ref)
        first = block.reshape(STATE, WIDE)
        second = (block * decay[None]).reshape(STATE, WIDE) + middle_ref[:, columns]
        own_ref[:, columns] = jnp.where(core == 0, first, second).astype(bf16)
        sent_ref[:, columns] = jnp.where(core == 0, second, first).astype(bf16)


def gated_part(place, starts_ref, half, base_ref, factor_ref, c_ref, state_ref, gated_ref, power):
    start = chunk_start(place, starts_ref, place % CORES)
    seen = iota((CHUNK, STATE), 0) < start
    for group in range(HALF):
        columns = pl.ds(pl.multiple_of(half * HALF_WIDE + group * WIDE, WIDE), WIDE)
        states = pl.ds(pl.multiple_of((half * HALF + group) * STATE, STATE), STATE)
        queries = jnp.where(seen, c_ref[:, states].astype(f32), 0.0).astype(bf16)
        here = slice(group * WIDE, (group + 1) * WIDE)
        outside = jnp.dot(queries, state_ref[:, here], preferred_element_type=f32)
        gated = base_ref[:, columns].astype(f32) + outside * factor_ref[:, columns].astype(f32)
        gated_ref[:, here] = gated
        squares = gated * gated
        for i in range(WIDE // LANES):
            power = power + squares[:, i * LANES : (i + 1) * LANES]
    return power


def own_kernel(place_ref, starts_ref, base_ref, factor_ref, c_ref, state_ref, gated_ref, power_ref):
    place = place_ref[0]
    power_ref[...] = gated_part(
        place, starts_ref, place % CORES, base_ref, factor_ref, c_ref, state_ref, gated_ref,
        jnp.zeros((CHUNK, LANES), f32),
    )


def last_kernel(
    place_ref, starts_ref, base_ref, factor_ref, c_ref, state_ref, gated_own_ref, power_own_ref, gain_ref,
    out_ref, gated_ref, done_ref, sems,
):
    place = place_ref[0]
    core = place % CORES
    power = gated_part(
        place, starts_ref, 1 - core, base_ref, factor_ref, c_ref, state_ref, gated_ref, power_own_ref[...]
    )
    total = jnp.sum(power, axis=1, keepdims=True)
    scale = lax.rsqrt(total * (1.0 / INNER) + EPS)
    rows = CHUNK // PARTS
    copies = []
    for part in range(PARTS):
        some = slice(part * rows, (part + 1) * rows)
        for half, ref in ((core, gated_own_ref), (1 - core, gated_ref)):
            columns = pl.ds(pl.multiple_of(half * HALF_WIDE, HALF_WIDE), HALF_WIDE)
            done_ref[some, columns] = (ref[some, :] * scale[some] * gain_ref[:, columns]).astype(bf16)
        copies.append(pltpu.make_async_copy(done_ref.at[some], out_ref.at[some], sems.at[part]))
        copies[-1].start()
    for copy in copies:
        copy.wait()


def local(
    head_inputs,
    gate_inputs,
    write_keys,
    read_queries,
    step_logits,
    step_bias,
    decay_log,
    skip_scale,
    norm_gain,
    document_starts,
):
    depth = lax.axis_size("z")
    blocks = lax.axis_size("ctx") * depth
    core = lax.axis_index("core")
    place = (lax.axis_index("z") * CORES + core).astype(jnp.int32).reshape(1)
    swap = [(0, 1), (1, 0)]
    devices = depth * CORES

    own = jnp.pad(jnp.stack([step_bias, decay_log, skip_scale]), ((0, SLAB - 3), (0, LANES - PER_GROUP)))
    turns = [
        lax.ppermute(
            own,
            ("z", "core"),
            [(HALF * (i % CORES) + (i // CORES + turn) % HALF, i) for i in range(devices)],
        )
        for turn in range(HALF)
    ]
    x_got = lax.ppermute(
        lax.dynamic_slice(head_inputs, (0, (1 - core) * HALF_WIDE), (CHUNK, HALF_WIDE)), "core", swap
    )
    b_got = lax.ppermute(
        lax.dynamic_slice(write_keys, (0, (1 - core) * HALF * STATE), (CHUNK, HALF * STATE)), "core", swap
    )
    logit_got = lax.ppermute(step_logits, "core", swap)

    smem = pl.BlockSpec(memory_space=pltpu.SMEM)
    vmem = pl.BlockSpec(memory_space=pltpu.VMEM)

    def call(kernel, scalars, operands, out_shape, scratch, name, cost=None, out_specs=None):
        return pl.pallas_call(
            kernel,
            in_specs=[smem] * len(scalars) + [vmem] * len(operands),
            out_specs=out_specs or [vmem] * len(out_shape),
            out_shape=out_shape,
            scratch_shapes=scratch,
            compiler_params=pltpu.CompilerParams(vmem_limit_bytes=24 * 2**20),
            cost_estimate=cost,
            name=name,
        )(*scalars, *operands)

    def shape(dims, kind):
        return jax.ShapeDtypeStruct(dims, kind)

    where = (place, document_starts)
    spread_scratch = pltpu.VMEM((2 * LANES, WIDE), bf16)

    pay, middle, params, decay = call(
        write_kernel,
        where,
        (*turns, step_logits, logit_got, head_inputs, x_got, write_keys, b_got),
        [
            shape((SLABS, HALF, SLAB, WIDE + LANES), bf16),
            shape((STATE, HALF_WIDE), f32),
            shape((SLAB, LANES), f32),
            shape((SLAB, LANES), f32),
        ],
        [spread_scratch],
        "write",
    )

    arrived = lax.all_to_all(
        pay.reshape(blocks, SLAB, WIDE + LANES), ("ctx", "z"), 0, 0, tiled=True
    )
    params_got = lax.ppermute(params, "core", swap)

    base, factor = call(
        inside_kernel,
        where,
        (params, params_got, step_logits, head_inputs, write_keys, read_queries, gate_inputs),
        [shape((CHUNK, INNER), bf16), shape((CHUNK, INNER), bf16)],
        [spread_scratch],
        "inside",
        pl.CostEstimate(flops=2 * 4 * CHUNK * STATE * INNER, bytes_accessed=9 * 2**20, transcendentals=2**20),
    )
    arrived, base, factor = lax.optimization_barrier((arrived, base, factor))

    [frozen] = call(
        functools.partial(scan_kernel, blocks),
        (),
        (arrived,),
        [shape((blocks, SLAB, WIDE), bf16)],
        [pltpu.VMEM((blocks, SLAB, WIDE), f32)],
        "scan",
    )

    returned = lax.all_to_all(frozen, ("ctx", "z"), 0, 0, tiled=True)

    half_state = shape((STATE, HALF_WIDE), bf16)
    state_own, state_sent = call(
        states_kernel,
        (place,),
        (returned.reshape(SLABS, HALF, SLAB, WIDE), middle, decay),
        [half_state, half_state],
        [spread_scratch],
        "states",
    )

    state_got = lax.ppermute(state_sent, "core", swap)

    gated, power = call(
        own_kernel,
        where,
        (base, factor, read_queries, state_own),
        [shape((CHUNK, HALF_WIDE), f32), shape((CHUNK, LANES), f32)],
        [],
        "own",
        pl.CostEstimate(flops=2 * CHUNK * STATE * INNER, bytes_accessed=5 * 2**20, transcendentals=0),
    )

    [out] = call(
        last_kernel,
        where,
        (base, factor, read_queries, state_got, gated, power, norm_gain.reshape(1, INNER)),
        [shape((CHUNK, INNER), bf16)],
        [
            pltpu.VMEM((CHUNK, HALF_WIDE), f32),
            pltpu.VMEM((CHUNK, INNER), bf16),
            pltpu.SemaphoreType.DMA((PARTS,)),
        ],
        "last",
        out_specs=[pl.BlockSpec(memory_space=pl.ANY)],
    )
    return out


def solution(mesh):
    ctx, head = mesh.devices.shape
    split = Mesh(mesh.devices.reshape(ctx, head // CORES, CORES), ("ctx", "z", "core"))
    tokens = P(("ctx", "z", "core"), None)
    return jax.shard_map(
        local,
        mesh=split,
        in_specs=(tokens,) * 5 + (P(("z", "core")),) * 3 + (P(), P("ctx")),
        out_specs=tokens,
        check_vma=False,
    )
```

```python
import functools

import jax
import jax.numpy as jnp
from jax import lax
from jax.experimental import pallas as pl
from jax.experimental.pallas import tpu as pltpu
from jax.sharding import Mesh
from jax.sharding import PartitionSpec as P

HEADS = 128
HEAD_DIM = 64
STATE = 128
GROUPS = 8
INNER = HEADS * HEAD_DIM
CHUNK = 128
CORES = 2
HALF = GROUPS // CORES
HALF_HEADS = HEADS // CORES
PER_GROUP = HEADS // GROUPS
WIDE = PER_GROUP * HEAD_DIM
HALF_WIDE = HALF * WIDE
SLAB = 8
SLABS = STATE // SLAB
LANES = 128
PARTS = 4
EPS = 1e-5

bf16 = jnp.bfloat16
f32 = jnp.float32


def iota(shape, axis):
    return lax.broadcasted_iota(jnp.int32, shape, axis)


def spreader(rows, parts):
    lane = iota((rows, WIDE), 0) % LANES
    head = iota((rows, WIDE), 1) // HEAD_DIM
    hit = (lane % PER_GROUP == head) & (lane < parts * PER_GROUP)
    return jnp.where(hit, 1.0, 0.0).astype(bf16)


def to_front(v, group):
    return pltpu.roll(v, (2 * LANES - PER_GROUP * group) % LANES, 1)


def spread(v, group, spread_ref):
    front = to_front(v, group)
    high = front.astype(bf16)
    low = (front - high.astype(f32)).astype(bf16)
    return jnp.dot(
        jnp.concatenate([high, low], axis=1), spread_ref[...], preferred_element_type=f32
    )


def from_front(v, group):
    return pltpu.roll(v, PER_GROUP * group, 1)


def columns_of(group, half, width):
    return pl.ds(pl.multiple_of((CORES * group + half) * width, width), width)


def softplus(v):
    return jnp.maximum(v, 0.0) + jnp.log1p(jnp.exp(-jnp.abs(v)))


def cumulated(step, decay):
    rate = -jnp.exp(decay) * step
    lower = jnp.where(iota((CHUNK, CHUNK), 0) >= iota((CHUNK, CHUNK), 1), 1.0, 0.0).astype(bf16)
    cum = jnp.zeros(rate.shape, f32)
    for _ in range(3):
        part = rate.astype(bf16)
        cum = cum + jnp.dot(lower, part, preferred_element_type=f32)
        rate = rate - part.astype(f32)
    return jnp.exp(cum), jnp.exp(-cum) * step


def chunk_start(place, starts_ref, core):
    begun = starts_ref[place // CORES] - core * CHUNK
    return jnp.where((begun >= 0) & (begun < CHUNK), begun, CHUNK)


def fetch(source, target, sem):
    copy = pltpu.make_async_copy(source, target, sem)
    copy.start()
    return copy


def pack_kernel(place_ref, bias_ref, decay_ref, skip_ref, logit_ref, x_ref, b_ref, packed_ref, own_ref, sems):
    core = place_ref[0] % CORES
    tail = HALF_WIDE + HALF * STATE
    copies = [fetch(logit_ref, packed_ref.at[:, pl.ds(tail, LANES)], sems.at[2 * HALF])]
    for group in range(HALF):
        to_x, to_key = pl.ds(group * WIDE, WIDE), pl.ds(HALF_WIDE + group * STATE, STATE)
        copies.append(fetch(x_ref.at[:, columns_of(group, 1 - core, WIDE)], packed_ref.at[:, to_x], sems.at[group]))
        copies.append(
            fetch(b_ref.at[:, columns_of(group, 1 - core, STATE)], packed_ref.at[:, to_key], sems.at[HALF + group])
        )
    own_ref[...] = jnp.zeros_like(own_ref)
    for i, ref in enumerate((bias_ref, decay_ref, skip_ref)):
        own_ref[i : i + 1, :PER_GROUP] = ref[...]
    for copy in copies:
        copy.wait()


def write_kernel(
    place_ref, starts_ref, own0, own1, own2, own3, logit_ref, got_ref, x_ref, b_ref,
    pay_out, middle_out, params_ref, decay_ref, pay_ref, middle_ref, spread_ref, sems,
):
    place = place_ref[0]
    core = place % CORES
    tail = HALF_WIDE + HALF * STATE
    spread_ref[...] = spreader(2 * LANES, 1)
    lane = iota((SLAB, LANES), 1)
    params = jnp.zeros((SLAB, LANES), f32)
    for turn, ref in enumerate((own0, own1, own2, own3)):
        some = jnp.where(lane < PER_GROUP, ref[...], 0.0)
        params = params + from_front(some, 2 * ((place // CORES + turn) % HALF) + core)
    params_ref[...] = params
    half = iota((CHUNK, LANES), 1) // PER_GROUP % CORES == core
    chunks = []
    for logit, of_core in ((logit_ref[...], core), (got_ref[:, tail:], 1 - core)):
        step = jnp.where(half, softplus(logit.astype(f32) + params[0:1]), 0.0)
        p, q = cumulated(step, params[1:2])
        start = chunk_start(place, starts_ref, of_core)
        last = jnp.broadcast_to(p[CHUNK - 1 : CHUNK, :], (SLAB, LANES))
        kept = (iota((CHUNK, STATE), 0) >= start) | (start >= CHUNK)
        chunks.append((q, last, jnp.where(start >= CHUNK, last, 0.0), kept))
    whole = chunks[0][2] * chunks[1][2]
    high = whole.astype(bf16).astype(f32)
    middle = (whole - high).astype(bf16).astype(f32)
    low = whole - high - middle
    second_decay = jnp.where(core == 0, chunks[1][2], chunks[0][2])
    decay_ref[...] = jnp.where(core == 0, chunks[0][2], chunks[1][2])

    sent = []
    for j in range(HALF):
        group = 2 * j + core
        columns = slice(j * WIDE, (j + 1) * WIDE)
        at = HALF_WIDE + j * STATE
        xs = (x_ref[:, columns_of(j, core, WIDE)], got_ref[:, columns])
        keys = (b_ref[:, columns_of(j, core, STATE)], got_ref[:, at : at + STATE])
        written = []
        for (q, last, _, kept), x, b in zip(chunks, xs, keys):
            xq = (x.astype(f32) * spread(q, group, spread_ref)).astype(bf16)
            b = jnp.where(kept, b.astype(f32), 0.0).astype(bf16)
            w = lax.dot_general(b, xq, (((0,), (0,)), ((), ())), preferred_element_type=f32)
            written.append(w.reshape(SLABS, SLAB, WIDE) * spread(last, group, spread_ref)[None])
        before = jnp.where(core == 0, written[0], written[1])
        after = jnp.where(core == 0, written[1], written[0])
        pay_ref[j, :, :, :WIDE] = (before * spread(second_decay, group, spread_ref)[None] + after).astype(bf16)
        packed = jnp.where(
            lane < PER_GROUP,
            to_front(high, group),
            jnp.where(
                lane < 2 * PER_GROUP,
                to_front(middle, group - 1),
                jnp.where(lane < 3 * PER_GROUP, to_front(low, group - 2), 0.0),
            ),
        ).astype(bf16)
        pay_ref[j, :, :, WIDE:] = jnp.broadcast_to(packed[None], (SLABS, SLAB, LANES))
        sent.append(fetch(pay_ref.at[j], pay_out.at[:, j], sems.at[0, j]))
        middle_ref[j] = before.reshape(STATE, WIDE)
        sent.append(fetch(middle_ref.at[j], middle_out.at[j], sems.at[1, j]))
    for copy in sent:
        copy.wait()


def scan_kernel(blocks, pay_ref, out_ref, carried_ref):
    packed = pay_ref[:, :, WIDE:].astype(f32).reshape(blocks * SLAB, LANES).astype(bf16)
    carried = jnp.dot(packed, spreader(LANES, 3), preferred_element_type=f32)
    carried_ref[...] = carried.reshape(blocks, SLAB, WIDE)

    def one(k, state):
        out_ref[k] = state.astype(bf16)
        return carried_ref[k] * state + pay_ref[k, :, :WIDE].astype(f32)

    lax.fori_loop(0, blocks, one, jnp.zeros((SLAB, WIDE), f32), unroll=8)


def inside_kernel(
    place_ref, starts_ref, params_ref, got_ref, x_ref, logit_in, b_in, c_in, gate_in,
    base_out, factor_out,
    logit_ref, b_ref, c_ref, gate_ref, base_ref, factor_ref, spread_ref, sems, sent_sems,
):
    place = place_ref[0]
    start = chunk_start(place, starts_ref, place % CORES)
    logit_copy = fetch(logit_in, logit_ref, sems.at[0])
    b_copy = fetch(b_in, b_ref, sems.at[1])
    c_copy = fetch(c_in, c_ref, sems.at[2])
    gate_copy = fetch(gate_in, gate_ref, sems.at[3])
    spread_ref[...] = spreader(2 * LANES, 1)
    params = params_ref[...] + got_ref[...]
    skips = jnp.broadcast_to(params[2:3], (SLAB, LANES))
    logit_copy.wait()
    step = softplus(logit_ref[...].astype(f32) + params[0:1])
    p, q = cumulated(step, params[1:2])
    t = iota((CHUNK, CHUNK), 0)
    s = iota((CHUNK, CHUNK), 1)
    allowed = (s <= t) & ((t >= start) == (s >= start))
    b_copy.wait()
    c_copy.wait()
    gate_copy.wait()
    sent = []
    for group in range(GROUPS):
        columns = slice(group * WIDE, (group + 1) * WIDE)
        states = slice(group * STATE, (group + 1) * STATE)
        x = x_ref[:, columns].astype(f32)
        xq = (x * spread(q, group, spread_ref)).astype(bf16)
        score = lax.dot_general(
            c_ref[:, states], b_ref[:, states], (((1,), (1,)), ((), ())), preferred_element_type=f32
        )
        mixing = jnp.where(allowed, score, 0.0).astype(bf16)
        inside = jnp.dot(mixing, xq, preferred_element_type=f32)
        skip = spread(skips, group, spread_ref)[:1]
        gate = gate_ref[:, columns].astype(f32)
        silu = gate / (1.0 + jnp.exp(-gate))
        grown = spread(p, group, spread_ref)
        base_ref[group] = ((inside * grown + skip * x) * silu).astype(bf16)
        factor_ref[group] = (grown * silu).astype(bf16)
        sent.append(fetch(base_ref.at[group], base_out.at[group], sent_sems.at[0, group]))
        sent.append(fetch(factor_ref.at[group], factor_out.at[group], sent_sems.at[1, group]))
    for copy in sent:
        copy.wait()


def states_kernel(place_ref, state_ref, middle_ref, decay_ref, own_ref, sent_ref, spread_ref):
    core = place_ref[0] % CORES
    spread_ref[...] = spreader(2 * LANES, 1)
    for group in range(HALF):
        columns = slice(group * WIDE, (group + 1) * WIDE)
        block = state_ref[:, group].astype(f32)
        decay = spread(decay_ref[...], 2 * group + core, spread_ref)
        first = block.reshape(STATE, WIDE)
        second = (block * decay[None]).reshape(STATE, WIDE) + middle_ref[group]
        own_ref[:, columns] = jnp.where(core == 0, first, second).astype(bf16)
        sent_ref[:, columns] = jnp.where(core == 0, second, first).astype(bf16)


def gated_part(place, starts_ref, half, base_ref, factor_ref, c_ref, state_ref, gated_ref, power):
    start = chunk_start(place, starts_ref, place % CORES)
    seen = iota((CHUNK, STATE), 0) < start
    for group in range(HALF):
        of_all = CORES * group + half
        states = columns_of(group, half, STATE)
        queries = jnp.where(seen, c_ref[:, states].astype(f32), 0.0).astype(bf16)
        here = slice(group * WIDE, (group + 1) * WIDE)
        outside = jnp.dot(queries, state_ref[:, here], preferred_element_type=f32)
        gated = base_ref[of_all].astype(f32) + outside * factor_ref[of_all].astype(f32)
        gated_ref[:, here] = gated
        squares = gated * gated
        for i in range(WIDE // LANES):
            power = power + squares[:, i * LANES : (i + 1) * LANES]
    return power


def own_kernel(place_ref, starts_ref, base_ref, factor_ref, c_ref, state_ref, gated_ref, power_ref):
    place = place_ref[0]
    power_ref[...] = gated_part(
        place, starts_ref, place % CORES, base_ref, factor_ref, c_ref, state_ref, gated_ref,
        jnp.zeros((CHUNK, LANES), f32),
    )


def last_kernel(
    place_ref, starts_ref, base_ref, factor_ref, c_ref, state_ref, gated_own_ref, power_own_ref, gain_ref,
    out_ref, gated_ref, done_ref, sems,
):
    place = place_ref[0]
    core = place % CORES
    power = gated_part(
        place, starts_ref, 1 - core, base_ref, factor_ref, c_ref, state_ref, gated_ref, power_own_ref[...]
    )
    total = jnp.sum(power, axis=1, keepdims=True)
    scale = lax.rsqrt(total * (1.0 / INNER) + EPS)
    rows = CHUNK // PARTS
    copies = []
    for part in range(PARTS):
        some = slice(part * rows, (part + 1) * rows)
        for half, ref in ((core, gated_own_ref), (1 - core, gated_ref)):
            for group in range(HALF):
                columns = columns_of(group, half, WIDE)
                gated = ref[some, group * WIDE : (group + 1) * WIDE]
                done_ref[some, columns] = (gated * scale[some] * gain_ref[:, columns]).astype(bf16)
        copies.append(pltpu.make_async_copy(done_ref.at[some], out_ref.at[some], sems.at[part]))
        copies[-1].start()
    for copy in copies:
        copy.wait()


def local(
    head_inputs,
    gate_inputs,
    write_keys,
    read_queries,
    step_logits,
    step_bias,
    decay_log,
    skip_scale,
    norm_gain,
    document_starts,
):
    depth = lax.axis_size("z")
    blocks = lax.axis_size("ctx") * depth
    core = lax.axis_index("core")
    place = (lax.axis_index("z") * CORES + core).astype(jnp.int32).reshape(1)
    swap = [(0, 1), (1, 0)]

    smem = pl.BlockSpec(memory_space=pltpu.SMEM)
    vmem = pl.BlockSpec(memory_space=pltpu.VMEM)

    anywhere = pl.BlockSpec(memory_space=pl.ANY)

    def call(kernel, scalars, operands, out_shape, scratch, name, cost=None, out_specs=None, in_specs=None, mib=24):
        return pl.pallas_call(
            kernel,
            in_specs=[smem] * len(scalars) + (in_specs or [vmem] * len(operands)),
            out_specs=out_specs or [vmem] * len(out_shape),
            out_shape=out_shape,
            scratch_shapes=scratch,
            compiler_params=pltpu.CompilerParams(vmem_limit_bytes=mib * 2**20),
            cost_estimate=cost,
            name=name,
        )(*scalars, *operands)

    def shape(dims, kind):
        return jax.ShapeDtypeStruct(dims, kind)

    where = (place, document_starts)
    spread_scratch = pltpu.VMEM((2 * LANES, WIDE), bf16)

    dma = pltpu.SemaphoreType.DMA
    packed_width = HALF_WIDE + HALF * STATE + LANES
    packed, own = call(
        pack_kernel,
        (place,),
        (
            *(v.reshape(1, PER_GROUP) for v in (step_bias, decay_log, skip_scale)),
            *(pltpu.with_memory_space_constraint(v, pltpu.HBM) for v in (step_logits, head_inputs, write_keys)),
        ),
        [pltpu.VMEM((CHUNK, packed_width), bf16), pltpu.VMEM((SLAB, LANES), f32)],
        [dma((2 * HALF + 1,))],
        "pack",
        in_specs=[vmem] * 3 + [anywhere] * 3,
    )
    turns = [own] + [
        lax.ppermute(own, "z", [((i + turn) % depth, i) for i in range(depth)]) for turn in range(1, HALF)
    ]
    packed_got = lax.ppermute(packed, "core", swap)

    pay, middle, params, decay = call(
        write_kernel,
        where,
        (*turns, step_logits, packed_got, head_inputs, write_keys),
        [
            pltpu.HBM((SLABS, HALF, SLAB, WIDE + LANES), bf16),
            pltpu.HBM((HALF, STATE, WIDE), f32),
            pltpu.VMEM((SLAB, LANES), f32),
            pltpu.VMEM((SLAB, LANES), f32),
        ],
        [
            pltpu.VMEM((HALF, SLABS, SLAB, WIDE + LANES), bf16),
            pltpu.VMEM((HALF, STATE, WIDE), f32),
            spread_scratch,
            dma((2, HALF)),
        ],
        "write",
        out_specs=[anywhere] * 2 + [vmem] * 2,
    )

    arrived = lax.all_to_all(
        pay.reshape(blocks, SLAB, WIDE + LANES), ("ctx", "z"), 0, 0, tiled=True
    )
    params_got = lax.ppermute(params, "core", swap)

    base, factor = call(
        inside_kernel,
        where,
        (
            params,
            params_got,
            head_inputs,
            *(
                pltpu.with_memory_space_constraint(v, pltpu.HBM)
                for v in (step_logits, write_keys, read_queries, gate_inputs)
            ),
        ),
        [pltpu.HBM((GROUPS, CHUNK, WIDE), bf16), pltpu.HBM((GROUPS, CHUNK, WIDE), bf16)],
        [
            pltpu.VMEM((CHUNK, LANES), bf16),
            pltpu.VMEM((CHUNK, GROUPS * STATE), bf16),
            pltpu.VMEM((CHUNK, GROUPS * STATE), bf16),
            pltpu.VMEM((CHUNK, INNER), bf16),
            pltpu.VMEM((GROUPS, CHUNK, WIDE), bf16),
            pltpu.VMEM((GROUPS, CHUNK, WIDE), bf16),
            spread_scratch,
            dma((4,)),
            dma((2, GROUPS)),
        ],
        "inside",
        pl.CostEstimate(flops=2 * 4 * CHUNK * STATE * INNER, bytes_accessed=9 * 2**20, transcendentals=2**20),
        out_specs=[anywhere] * 2,
        in_specs=[vmem] * 3 + [anywhere] * 4,
    )
    arrived, base, factor = lax.optimization_barrier((arrived, base, factor))

    [frozen] = call(
        functools.partial(scan_kernel, blocks),
        (),
        (arrived,),
        [shape((blocks, SLAB, WIDE), bf16)],
        [pltpu.VMEM((blocks, SLAB, WIDE), f32)],
        "scan",
    )

    returned = lax.all_to_all(frozen, ("ctx", "z"), 0, 0, tiled=True)

    half_state = shape((STATE, HALF_WIDE), bf16)
    state_own, state_sent = call(
        states_kernel,
        (place,),
        (returned.reshape(SLABS, HALF, SLAB, WIDE), middle, decay),
        [half_state, half_state],
        [spread_scratch],
        "states",
    )

    state_got = lax.ppermute(state_sent, "core", swap)

    gated, power = call(
        own_kernel,
        where,
        (base, factor, read_queries, state_own),
        [shape((CHUNK, HALF_WIDE), f32), shape((CHUNK, LANES), f32)],
        [],
        "own",
        pl.CostEstimate(flops=2 * CHUNK * STATE * INNER, bytes_accessed=5 * 2**20, transcendentals=0),
    )

    [out] = call(
        last_kernel,
        where,
        (base, factor, read_queries, state_got, gated, power, norm_gain.reshape(1, INNER)),
        [shape((CHUNK, INNER), bf16)],
        [
            pltpu.VMEM((CHUNK, HALF_WIDE), f32),
            pltpu.VMEM((CHUNK, INNER), bf16),
            pltpu.SemaphoreType.DMA((PARTS,)),
        ],
        "last",
        out_specs=[pl.BlockSpec(memory_space=pl.ANY)],
    )
    return out


def solution(mesh):
    ctx, head = mesh.devices.shape
    split = Mesh(mesh.devices.reshape(ctx, head // CORES, CORES), ("ctx", "z", "core"))
    tokens = P(("ctx", "z", "core"), None)
    return jax.shard_map(
        local,
        mesh=split,
        in_specs=(tokens,) * 5 + (P(("z", "core")),) * 3 + (P(), P("ctx")),
        out_specs=tokens,
        check_vma=False,
    )
```

```python
import functools

import jax
import jax.numpy as jnp
from jax import lax
from jax.experimental import pallas as pl
from jax.experimental.pallas import tpu as pltpu
from jax.sharding import Mesh
from jax.sharding import PartitionSpec as P

HEADS = 128
HEAD_DIM = 64
STATE = 128
GROUPS = 8
INNER = HEADS * HEAD_DIM
CHUNK = 128
CORES = 2
HALF = GROUPS // CORES
HALF_HEADS = HEADS // CORES
PER_GROUP = HEADS // GROUPS
WIDE = PER_GROUP * HEAD_DIM
HALF_WIDE = HALF * WIDE
SLAB = 8
SLABS = STATE // SLAB
LANES = 128
PIECE = 4
PARTS = 4
EPS = 1e-5

bf16 = jnp.bfloat16
f32 = jnp.float32


def iota(shape, axis):
    return lax.broadcasted_iota(jnp.int32, shape, axis)


def spreader(rows, parts):
    lane = iota((rows, WIDE), 0) % LANES
    head = iota((rows, WIDE), 1) // HEAD_DIM
    hit = (lane % PER_GROUP == head) & (lane < parts * PER_GROUP)
    return jnp.where(hit, 1.0, 0.0).astype(bf16)


def to_front(v, group):
    return pltpu.roll(v, (2 * LANES - PER_GROUP * group) % LANES, 1)


def spread(v, group, spread_ref):
    front = to_front(v, group)
    high = front.astype(bf16)
    low = (front - high.astype(f32)).astype(bf16)
    return jnp.dot(
        jnp.concatenate([high, low], axis=1), spread_ref[...], preferred_element_type=f32
    )


def from_front(v, group):
    return pltpu.roll(v, PER_GROUP * group, 1)


def columns_of(group, half, width):
    return pl.ds(pl.multiple_of((CORES * group + half) * width, width), width)


def softplus(v):
    return jnp.maximum(v, 0.0) + jnp.log1p(jnp.exp(-jnp.abs(v)))


def cumulated(step, decay):
    rate = -jnp.exp(decay) * step
    lower = iota((CHUNK, 3 * CHUNK), 0) >= iota((CHUNK, 3 * CHUNK), 1) % CHUNK
    parts = []
    for _ in range(3):
        parts.append(rate.astype(bf16))
        rate = rate - parts[-1].astype(f32)
    cum = jnp.dot(
        jnp.where(lower, 1.0, 0.0).astype(bf16), jnp.concatenate(parts, axis=0), preferred_element_type=f32
    )
    return jnp.exp(cum), jnp.exp(-cum) * step


def chunk_start(place, starts_ref, core):
    begun = starts_ref[place // CORES] - core * CHUNK
    return jnp.where((begun >= 0) & (begun < CHUNK), begun, CHUNK)


def fetch(source, target, sem):
    copy = pltpu.make_async_copy(source, target, sem)
    copy.start()
    return copy


def pack_kernel(
    place_ref, bias_in, decay_in, skip_in, logit_ref, x_ref, b_ref, packed_ref, own_ref, spread_ref,
    bias_ref, decay_ref, skip_ref, sems, row_sems,
):
    core = place_ref[0] % CORES
    tail = HALF_WIDE + HALF * STATE
    rows = [
        fetch(source, target, row_sems.at[i])
        for i, (source, target) in enumerate(
            ((bias_in, bias_ref), (decay_in, decay_ref), (skip_in, skip_ref))
        )
    ]
    copies = [fetch(logit_ref, packed_ref.at[:, pl.ds(tail, LANES)], sems.at[2 * HALF])]
    for group in range(HALF):
        to_x, to_key = pl.ds(group * WIDE, WIDE), pl.ds(HALF_WIDE + group * STATE, STATE)
        copies.append(fetch(x_ref.at[:, columns_of(group, 1 - core, WIDE)], packed_ref.at[:, to_x], sems.at[group]))
        copies.append(
            fetch(b_ref.at[:, columns_of(group, 1 - core, STATE)], packed_ref.at[:, to_key], sems.at[HALF + group])
        )
    spread_ref[...] = spreader(2 * LANES, 1)
    own_ref[...] = jnp.zeros_like(own_ref)
    for i, ref in enumerate((bias_ref, decay_ref, skip_ref)):
        rows[i].wait()
        own_ref[i : i + 1, :PER_GROUP] = ref[...]
    for copy in copies:
        copy.wait()


def write_kernel(
    place_ref, starts_ref, own0, own1, own2, own3, spread_ref, logit_ref, got_ref, x_ref, b_ref,
    pay_out, middle_out, params_ref, pay_ref, middle_ref, sems,
):
    place = place_ref[0]
    core = place % CORES
    tail = HALF_WIDE + HALF * STATE
    lane = iota((SLAB, LANES), 1)
    params = jnp.zeros((SLAB, LANES), f32)
    for turn, ref in enumerate((own0, own1, own2, own3)):
        some = jnp.where(lane < PER_GROUP, ref[...], 0.0)
        params = params + from_front(some, 2 * ((place // CORES + turn) % HALF) + core)
    params_ref[...] = params
    logit = jnp.concatenate([logit_ref[...].astype(f32), got_ref[:, tail:].astype(f32)], axis=1)
    half = iota((CHUNK, 2 * LANES), 1) // PER_GROUP % CORES == core
    both = jnp.concatenate([params, params], axis=1)
    step = jnp.where(half, softplus(logit + both[0:1]), 0.0)
    p, q = cumulated(step, both[1:2])
    last = jnp.broadcast_to(p[CHUNK - 1 : CHUNK], (SLAB, 2 * LANES))
    rows = jnp.concatenate([q[:, :LANES], q[:, LANES:], last[:, :LANES], last[:, LANES:]], axis=0)
    starts = (chunk_start(place, starts_ref, core), chunk_start(place, starts_ref, 1 - core))
    open_ = (starts[0] >= CHUNK, starts[1] >= CHUNK)
    kept = [(iota((CHUNK, STATE), 0) >= start) | (start >= CHUNK) for start in starts]
    whole = jnp.where(open_[0] & open_[1], last[:, :LANES] * last[:, LANES:], 0.0)
    high = whole.astype(bf16).astype(f32)
    middle = (whole - high).astype(bf16).astype(f32)
    low = whole - high - middle

    sent = []
    for j in range(HALF):
        group = 2 * j + core
        columns = slice(j * WIDE, (j + 1) * WIDE)
        at = HALF_WIDE + j * STATE
        xs = (x_ref[:, columns_of(j, core, WIDE)], got_ref[:, columns])
        keys = (b_ref[:, columns_of(j, core, STATE)], got_ref[:, at : at + STATE])
        wide = spread(rows, group, spread_ref)
        lasts = (wide[2 * CHUNK : 2 * CHUNK + SLAB], wide[2 * CHUNK + SLAB :])
        written = []
        for i in range(2):
            xq = (xs[i].astype(f32) * wide[i * CHUNK : (i + 1) * CHUNK]).astype(bf16)
            b = jnp.where(kept[i], keys[i].astype(f32), 0.0).astype(bf16)
            w = lax.dot_general(b, xq, (((0,), (0,)), ((), ())), preferred_element_type=f32)
            written.append(w.reshape(SLABS, SLAB, WIDE) * lasts[i][None])
        decays = [jnp.where(open_[i], lasts[i], 0.0) for i in range(2)]
        second = jnp.where(core == 0, decays[1], decays[0])
        before = jnp.where(core == 0, written[0], written[1])
        after = jnp.where(core == 0, written[1], written[0])
        pay_ref[j, :, :, :WIDE] = (before * second[None] + after).astype(bf16)
        packed = jnp.where(
            lane < PER_GROUP,
            to_front(high, group),
            jnp.where(
                lane < 2 * PER_GROUP,
                to_front(middle, group - 1),
                jnp.where(lane < 3 * PER_GROUP, to_front(low, group - 2), 0.0),
            ),
        ).astype(bf16)
        pay_ref[j, :, :, WIDE:] = jnp.broadcast_to(packed[None], (SLABS, SLAB, LANES))
        sent.append(fetch(pay_ref.at[j], pay_out.at[:, j], sems.at[0, j]))
        middle_ref[j, :STATE] = before.reshape(STATE, WIDE)
        middle_ref[j, STATE:] = jnp.where(core == 0, decays[0], decays[1])
        sent.append(fetch(middle_ref.at[j], middle_out.at[j], sems.at[1, j]))
    for copy in sent:
        copy.wait()


def scan_kernel(blocks, pay_ref, out_ref, carried_ref):
    packed = pay_ref[:, :, WIDE:].astype(f32).reshape(blocks * SLAB, LANES).astype(bf16)
    carried = jnp.dot(packed, spreader(LANES, 3), preferred_element_type=f32)
    carried_ref[...] = carried.reshape(blocks, SLAB, WIDE)

    def one(k, state):
        out_ref[k] = state.astype(bf16)
        return carried_ref[k] * state + pay_ref[k, :, :WIDE].astype(f32)

    lax.fori_loop(0, blocks, one, jnp.zeros((SLAB, WIDE), f32), unroll=8)


def inside_kernel(
    place_ref, starts_ref, params_ref, got_ref, x_ref, logit_in, b_in, c_in, gate_in,
    base_out, factor_out,
    logit_ref, b_ref, c_ref, gate_ref, base_ref, factor_ref, spread_ref, sems, sent_sems,
):
    place = place_ref[0]
    start = chunk_start(place, starts_ref, place % CORES)
    logit_copy = fetch(logit_in, logit_ref, sems.at[0])
    b_copy = fetch(b_in, b_ref, sems.at[1])
    c_copy = fetch(c_in, c_ref, sems.at[2])
    gate_copy = fetch(gate_in, gate_ref, sems.at[3])
    spread_ref[...] = spreader(2 * LANES, 1)
    params = params_ref[...] + got_ref[...]
    logit_copy.wait()
    step = softplus(logit_ref[...].astype(f32) + params[0:1])
    p, q = cumulated(step, params[1:2])
    rows = jnp.concatenate([q, p, jnp.broadcast_to(params[2:3], (2 * SLAB, LANES))], axis=0)
    t = iota((CHUNK, CHUNK), 0)
    s = iota((CHUNK, CHUNK), 1)
    allowed = (s <= t) & ((t >= start) == (s >= start))
    b_copy.wait()
    c_copy.wait()
    gate_copy.wait()
    sent = []
    for group in range(GROUPS):
        columns = slice(group * WIDE, (group + 1) * WIDE)
        states = slice(group * STATE, (group + 1) * STATE)
        wide = spread(rows, group, spread_ref)
        grown = wide[CHUNK : 2 * CHUNK]
        x = x_ref[:, columns].astype(f32)
        xq = (x * wide[:CHUNK]).astype(bf16)
        score = lax.dot_general(
            c_ref[:, states], b_ref[:, states], (((1,), (1,)), ((), ())), preferred_element_type=f32
        )
        mixing = jnp.where(allowed, score, 0.0).astype(bf16)
        inside = jnp.dot(mixing, xq, preferred_element_type=f32)
        skip = wide[2 * CHUNK : 2 * CHUNK + 1]
        gate = gate_ref[:, columns].astype(f32)
        silu = gate / (1.0 + jnp.exp(-gate))
        base_ref[group] = ((inside * grown + skip * x) * silu).astype(bf16)
        factor_ref[group] = (grown * silu).astype(bf16)
        sent.append(fetch(base_ref.at[group], base_out.at[group], sent_sems.at[0, group]))
        sent.append(fetch(factor_ref.at[group], factor_out.at[group], sent_sems.at[1, group]))
    for copy in sent:
        copy.wait()


def states_kernel(first_group, place_ref, state_ref, middle_ref, own_ref, sent_ref):
    core = place_ref[0] % CORES
    for i in range(PIECE):
        group = first_group + i
        block = state_ref[:, group].astype(f32)
        first = block.reshape(STATE, WIDE)
        second = (block * middle_ref[group, STATE:][None]).reshape(STATE, WIDE) + middle_ref[group, :STATE]
        own_ref[i] = jnp.where(core == 0, first, second).astype(bf16)
        sent_ref[i] = jnp.where(core == 0, second, first).astype(bf16)


def gated_part(place, starts_ref, half, first_group, base_ref, factor_ref, c_ref, state_ref, gated_ref, power):
    start = chunk_start(place, starts_ref, place % CORES)
    seen = iota((CHUNK, STATE), 0) < start
    for i in range(PIECE):
        group = first_group + i
        of_all = CORES * group + half
        queries = jnp.where(seen, c_ref[:, columns_of(group, half, STATE)].astype(f32), 0.0).astype(bf16)
        outside = jnp.dot(queries, state_ref[i], preferred_element_type=f32)
        gated = base_ref[of_all].astype(f32) + outside * factor_ref[of_all].astype(f32)
        gated_ref[group] = gated
        squares = gated * gated
        for k in range(WIDE // LANES):
            power = power + squares[:, k * LANES : (k + 1) * LANES]
    return power


def own_kernel(place_ref, starts_ref, base_ref, factor_ref, c_ref, *refs):
    *states, gated_ref, power_ref = refs
    place = place_ref[0]
    power = jnp.zeros((CHUNK, LANES), f32)
    for i, state_ref in enumerate(states):
        power = gated_part(
            place, starts_ref, place % CORES, i * PIECE, base_ref, factor_ref, c_ref, state_ref, gated_ref, power
        )
    power_ref[...] = power


def last_kernel(
    place_ref, starts_ref, base_ref, factor_ref, c_ref, *refs
):
    *states, gated_own_ref, power_own_ref, gain_ref, out_ref, gated_ref, done_ref, sems = refs
    place = place_ref[0]
    core = place % CORES
    power = power_own_ref[...]
    for i, state_ref in enumerate(states):
        power = gated_part(
            place, starts_ref, 1 - core, i * PIECE, base_ref, factor_ref, c_ref, state_ref, gated_ref, power
        )
    total = jnp.sum(power, axis=1, keepdims=True)
    scale = lax.rsqrt(total * (1.0 / INNER) + EPS)
    rows = CHUNK // PARTS
    copies = []
    for part in range(PARTS):
        some = slice(part * rows, (part + 1) * rows)
        for half, ref in ((core, gated_own_ref), (1 - core, gated_ref)):
            for group in range(HALF):
                columns = columns_of(group, half, WIDE)
                gated = ref[group, some]
                done_ref[some, columns] = (gated * scale[some] * gain_ref[:, columns]).astype(bf16)
        copies.append(fetch(done_ref.at[some], out_ref.at[some], sems.at[part]))
    for copy in copies:
        copy.wait()


def local(
    head_inputs,
    gate_inputs,
    write_keys,
    read_queries,
    step_logits,
    step_bias,
    decay_log,
    skip_scale,
    norm_gain,
    document_starts,
):
    depth = lax.axis_size("z")
    blocks = lax.axis_size("ctx") * depth
    core = lax.axis_index("core")
    place = (lax.axis_index("z") * CORES + core).astype(jnp.int32).reshape(1)
    swap = [(0, 1), (1, 0)]

    smem = pl.BlockSpec(memory_space=pltpu.SMEM)
    vmem = pl.BlockSpec(memory_space=pltpu.VMEM)

    anywhere = pl.BlockSpec(memory_space=pl.ANY)

    def call(kernel, scalars, operands, out_shape, scratch, name, cost=None, out_specs=None, in_specs=None, mib=24):
        return pl.pallas_call(
            kernel,
            in_specs=[smem] * len(scalars) + (in_specs or [vmem] * len(operands)),
            out_specs=out_specs or [vmem] * len(out_shape),
            out_shape=out_shape,
            scratch_shapes=scratch,
            compiler_params=pltpu.CompilerParams(vmem_limit_bytes=mib * 2**20),
            cost_estimate=cost,
            name=name,
        )(*scalars, *operands)

    def shape(dims, kind):
        return jax.ShapeDtypeStruct(dims, kind)

    where = (place, document_starts)
    spread_scratch = pltpu.VMEM((2 * LANES, WIDE), bf16)

    dma = pltpu.SemaphoreType.DMA
    packed_width = HALF_WIDE + HALF * STATE + LANES
    packed, own, spread_matrix = call(
        pack_kernel,
        (place,),
        (
            *(
                pltpu.with_memory_space_constraint(v, pltpu.HBM)
                for v in (
                    *(v.reshape(1, PER_GROUP) for v in (step_bias, decay_log, skip_scale)),
                    step_logits,
                    head_inputs,
                    write_keys,
                )
            ),
        ),
        [
            pltpu.VMEM((CHUNK, packed_width), bf16),
            pltpu.VMEM((SLAB, LANES), f32),
            pltpu.VMEM((2 * LANES, WIDE), bf16),
        ],
        [pltpu.VMEM((1, PER_GROUP), f32)] * 3 + [dma((2 * HALF + 1,)), dma((3,))],
        "pack",
        in_specs=[anywhere] * 6,
    )
    turns = [own] + [
        lax.ppermute(own, "z", [((i + turn) % depth, i) for i in range(depth)]) for turn in range(1, HALF)
    ]
    packed_got = lax.ppermute(packed, "core", swap)

    pay, middle, params = call(
        write_kernel,
        where,
        (*turns, spread_matrix, step_logits, packed_got, head_inputs, write_keys),
        [
            pltpu.HBM((SLABS, HALF, SLAB, WIDE + LANES), bf16),
            pltpu.HBM((HALF, STATE + SLAB, WIDE), f32),
            pltpu.VMEM((SLAB, LANES), f32),
        ],
        [
            pltpu.VMEM((HALF, SLABS, SLAB, WIDE + LANES), bf16),
            pltpu.VMEM((HALF, STATE + SLAB, WIDE), f32),
            dma((2, HALF)),
        ],
        "write",
        out_specs=[anywhere] * 2 + [vmem],
    )

    arrived = lax.all_to_all(
        pay.reshape(blocks, SLAB, WIDE + LANES), ("ctx", "z"), 0, 0, tiled=True
    )
    params_got = lax.ppermute(params, "core", swap)

    base, factor = call(
        inside_kernel,
        where,
        (
            params,
            params_got,
            head_inputs,
            *(
                pltpu.with_memory_space_constraint(v, pltpu.HBM)
                for v in (step_logits, write_keys, read_queries, gate_inputs)
            ),
        ),
        [pltpu.HBM((GROUPS, CHUNK, WIDE), bf16), pltpu.HBM((GROUPS, CHUNK, WIDE), bf16)],
        [
            pltpu.VMEM((CHUNK, LANES), bf16),
            pltpu.VMEM((CHUNK, GROUPS * STATE), bf16),
            pltpu.VMEM((CHUNK, GROUPS * STATE), bf16),
            pltpu.VMEM((CHUNK, INNER), bf16),
            pltpu.VMEM((GROUPS, CHUNK, WIDE), bf16),
            pltpu.VMEM((GROUPS, CHUNK, WIDE), bf16),
            spread_scratch,
            dma((4,)),
            dma((2, GROUPS)),
        ],
        "inside",
        pl.CostEstimate(flops=2 * 4 * CHUNK * STATE * INNER, bytes_accessed=9 * 2**20, transcendentals=2**20),
        out_specs=[anywhere] * 2,
        in_specs=[vmem] * 3 + [anywhere] * 4,
    )
    arrived, base, factor = lax.optimization_barrier((arrived, base, factor))

    [frozen] = call(
        functools.partial(scan_kernel, blocks),
        (),
        (arrived,),
        [shape((blocks, SLAB, WIDE), bf16)],
        [pltpu.VMEM((blocks, SLAB, WIDE), f32)],
        "scan",
    )

    returned = lax.all_to_all(frozen, ("ctx", "z"), 0, 0, tiled=True)

    piece_state = shape((PIECE, STATE, WIDE), bf16)
    states_own, states_sent = [], []
    for first_group in range(0, HALF, PIECE):
        one, other = call(
            functools.partial(states_kernel, first_group),
            (place,),
            (returned.reshape(SLABS, HALF, SLAB, WIDE), middle),
            [piece_state, piece_state],
            [],
            "states",
        )
        states_own.append(one)
        states_sent.append(other)
    states_got = [lax.ppermute(v, "core", swap) for v in states_sent]

    gated, power = call(
        own_kernel,
        where,
        (base, factor, read_queries, *states_own),
        [shape((HALF, CHUNK, WIDE), f32), shape((CHUNK, LANES), f32)],
        [],
        "own",
        pl.CostEstimate(flops=2 * CHUNK * STATE * INNER, bytes_accessed=5 * 2**20, transcendentals=0),
    )

    [out] = call(
        last_kernel,
        where,
        (base, factor, read_queries, *states_got, gated, power, norm_gain.reshape(1, INNER)),
        [shape((CHUNK, INNER), bf16)],
        [
            pltpu.VMEM((HALF, CHUNK, WIDE), f32),
            pltpu.VMEM((CHUNK, INNER), bf16),
            dma((PARTS,)),
        ],
        "last",
        out_specs=[anywhere],
    )
    return out


def solution(mesh):
    ctx, head = mesh.devices.shape
    split = Mesh(mesh.devices.reshape(ctx, head // CORES, CORES), ("ctx", "z", "core"))
    tokens = P(("ctx", "z", "core"), None)
    return jax.shard_map(
        local,
        mesh=split,
        in_specs=(tokens,) * 5 + (P(("z", "core")),) * 3 + (P(), P("ctx")),
        out_specs=tokens,
        check_vma=False,
    )
```

```python
import functools

import jax
import jax.numpy as jnp
from jax import lax
from jax.experimental import pallas as pl
from jax.experimental.pallas import tpu as pltpu
from jax.sharding import Mesh
from jax.sharding import PartitionSpec as P

HEADS = 128
HEAD_DIM = 64
STATE = 128
GROUPS = 8
INNER = HEADS * HEAD_DIM
CHUNK = 128
CORES = 2
HALF = GROUPS // CORES
HALF_HEADS = HEADS // CORES
PER_GROUP = HEADS // GROUPS
WIDE = PER_GROUP * HEAD_DIM
HALF_WIDE = HALF * WIDE
SLAB = 8
SLABS = STATE // SLAB
LANES = 128
PIECE = 4
AHEAD = 6
PARTS = 4
EPS = 1e-5

bf16 = jnp.bfloat16
f32 = jnp.float32


def iota(shape, axis):
    return lax.broadcasted_iota(jnp.int32, shape, axis)


def spreader(rows, parts):
    lane = iota((rows, WIDE), 0) % LANES
    head = iota((rows, WIDE), 1) // HEAD_DIM
    hit = (lane % PER_GROUP == head) & (lane < parts * PER_GROUP)
    return jnp.where(hit, 1.0, 0.0).astype(bf16)


def to_front(v, group):
    return pltpu.roll(v, (2 * LANES - PER_GROUP * group) % LANES, 1)


def spread(v, group, spread_ref):
    front = to_front(v, group)
    high = front.astype(bf16)
    low = (front - high.astype(f32)).astype(bf16)
    return jnp.dot(
        jnp.concatenate([high, low], axis=1), spread_ref[...], preferred_element_type=f32
    )


def from_front(v, group):
    return pltpu.roll(v, PER_GROUP * group, 1)


def columns_of(group, half, width):
    return pl.ds(pl.multiple_of((CORES * group + half) * width, width), width)


def softplus(v):
    return jnp.maximum(v, 0.0) + jnp.log1p(jnp.exp(-jnp.abs(v)))


def cumulated(step, decay):
    rate = -jnp.exp(decay) * step
    lower = iota((CHUNK, 3 * CHUNK), 0) >= iota((CHUNK, 3 * CHUNK), 1) % CHUNK
    parts = []
    for _ in range(3):
        parts.append(rate.astype(bf16))
        rate = rate - parts[-1].astype(f32)
    cum = jnp.dot(
        jnp.where(lower, 1.0, 0.0).astype(bf16), jnp.concatenate(parts, axis=0), preferred_element_type=f32
    )
    return jnp.exp(cum), jnp.exp(-cum) * step


def chunk_start(place, starts_ref, core):
    begun = starts_ref[place // CORES] - core * CHUNK
    return jnp.where((begun >= 0) & (begun < CHUNK), begun, CHUNK)


def fetch(source, target, sem):
    copy = pltpu.make_async_copy(source, target, sem)
    copy.start()
    return copy


def placed(turn_rows, place, core):
    lane = iota((SLAB, LANES), 1)
    params = jnp.zeros((SLAB, LANES), f32)
    for turn, rows in enumerate(turn_rows):
        some = jnp.where(lane < PER_GROUP, rows, 0.0)
        params = params + from_front(some, 2 * ((place // CORES + turn) % HALF) + core)
    return params


def allowed_pairs(start):
    t = iota((CHUNK, CHUNK), 0)
    s = iota((CHUNK, CHUNK), 1)
    return (s <= t) & ((t >= start) == (s >= start))


def group_terms(rows, group, spread_ref, allowed, x, keys, queries, gate):
    wide = spread(rows, group, spread_ref)
    grown = wide[CHUNK : 2 * CHUNK]
    x = x.astype(f32)
    xq = (x * wide[:CHUNK]).astype(bf16)
    score = lax.dot_general(queries, keys, (((1,), (1,)), ((), ())), preferred_element_type=f32)
    mixing = jnp.where(allowed, score, 0.0).astype(bf16)
    inside = jnp.dot(mixing, xq, preferred_element_type=f32)
    skip = wide[2 * CHUNK : 2 * CHUNK + 1]
    gate = gate.astype(f32)
    silu = gate / (1.0 + jnp.exp(-gate))
    return ((inside * grown + skip * x) * silu).astype(bf16), (grown * silu).astype(bf16)


def pack_kernel(
    place_ref, bias_in, decay_in, skip_in, logit_ref, x_ref, b_ref, packed_ref, own_ref, spread_ref,
    bias_ref, decay_ref, skip_ref, sems, row_sems,
):
    core = place_ref[0] % CORES
    tail = HALF_WIDE + HALF * STATE
    rows = [
        fetch(source, target, row_sems.at[i])
        for i, (source, target) in enumerate(
            ((bias_in, bias_ref), (decay_in, decay_ref), (skip_in, skip_ref))
        )
    ]
    copies = [fetch(logit_ref, packed_ref.at[:, pl.ds(tail, LANES)], sems.at[2 * HALF])]
    for group in range(HALF):
        to_x, to_key = pl.ds(group * WIDE, WIDE), pl.ds(HALF_WIDE + group * STATE, STATE)
        copies.append(fetch(x_ref.at[:, columns_of(group, 1 - core, WIDE)], packed_ref.at[:, to_x], sems.at[group]))
        copies.append(
            fetch(b_ref.at[:, columns_of(group, 1 - core, STATE)], packed_ref.at[:, to_key], sems.at[HALF + group])
        )
    spread_ref[...] = spreader(2 * LANES, 1)
    own_ref[...] = jnp.zeros_like(own_ref)
    for i, ref in enumerate((bias_ref, decay_ref, skip_ref)):
        rows[i].wait()
        own_ref[i : i + 1, :PER_GROUP] = ref[...]
    for copy in copies:
        copy.wait()


def write_kernel(
    place_ref, starts_ref, own0, own1, own2, own3, spread_ref, logit_ref, got_ref, x_ref, b_ref,
    pay_out, middle_out, pay_ref, middle_ref, sems,
):
    place = place_ref[0]
    core = place % CORES
    tail = HALF_WIDE + HALF * STATE
    lane = iota((SLAB, LANES), 1)
    params = placed([ref[...] for ref in (own0, own1, own2, own3)], place, core)
    logit = jnp.concatenate([logit_ref[...].astype(f32), got_ref[:, tail:].astype(f32)], axis=1)
    half = iota((CHUNK, 2 * LANES), 1) // PER_GROUP % CORES == core
    both = jnp.concatenate([params, params], axis=1)
    step = jnp.where(half, softplus(logit + both[0:1]), 0.0)
    p, q = cumulated(step, both[1:2])
    last = jnp.broadcast_to(p[CHUNK - 1 : CHUNK], (SLAB, 2 * LANES))
    rows = jnp.concatenate([q[:, :LANES], q[:, LANES:], last[:, :LANES], last[:, LANES:]], axis=0)
    starts = (chunk_start(place, starts_ref, core), chunk_start(place, starts_ref, 1 - core))
    open_ = (starts[0] >= CHUNK, starts[1] >= CHUNK)
    kept = [(iota((CHUNK, STATE), 0) >= start) | (start >= CHUNK) for start in starts]
    whole = jnp.where(open_[0] & open_[1], last[:, :LANES] * last[:, LANES:], 0.0)
    high = whole.astype(bf16).astype(f32)
    middle = (whole - high).astype(bf16).astype(f32)
    low = whole - high - middle

    sent = []
    for j in range(HALF):
        group = 2 * j + core
        columns = slice(j * WIDE, (j + 1) * WIDE)
        at = HALF_WIDE + j * STATE
        xs = (x_ref[:, columns_of(j, core, WIDE)], got_ref[:, columns])
        keys = (b_ref[:, columns_of(j, core, STATE)], got_ref[:, at : at + STATE])
        wide = spread(rows, group, spread_ref)
        lasts = (wide[2 * CHUNK : 2 * CHUNK + SLAB], wide[2 * CHUNK + SLAB :])
        written = []
        for i in range(2):
            xq = (xs[i].astype(f32) * wide[i * CHUNK : (i + 1) * CHUNK]).astype(bf16)
            b = jnp.where(kept[i], keys[i].astype(f32), 0.0).astype(bf16)
            w = lax.dot_general(b, xq, (((0,), (0,)), ((), ())), preferred_element_type=f32)
            written.append(w.reshape(SLABS, SLAB, WIDE) * lasts[i][None])
        decays = [jnp.where(open_[i], lasts[i], 0.0) for i in range(2)]
        second = jnp.where(core == 0, decays[1], decays[0])
        before = jnp.where(core == 0, written[0], written[1])
        after = jnp.where(core == 0, written[1], written[0])
        pay_ref[j, :, :, :WIDE] = (before * second[None] + after).astype(bf16)
        packed = jnp.where(
            lane < PER_GROUP,
            to_front(high, group),
            jnp.where(
                lane < 2 * PER_GROUP,
                to_front(middle, group - 1),
                jnp.where(lane < 3 * PER_GROUP, to_front(low, group - 2), 0.0),
            ),
        ).astype(bf16)
        pay_ref[j, :, :, WIDE:] = jnp.broadcast_to(packed[None], (SLABS, SLAB, LANES))
        sent.append(fetch(pay_ref.at[j], pay_out.at[:, j], sems.at[0, j]))
        middle_ref[j, :STATE] = before.reshape(STATE, WIDE)
        middle_ref[j, STATE:] = jnp.where(core == 0, decays[0], decays[1])
        sent.append(fetch(middle_ref.at[j], middle_out.at[j], sems.at[1, j]))
    for copy in sent:
        copy.wait()


def scan_kernel(blocks, pay_ref, out_ref, carried_ref):
    packed = pay_ref[:, :, WIDE:].astype(f32).reshape(blocks * SLAB, LANES).astype(bf16)
    carried = jnp.dot(packed, spreader(LANES, 3), preferred_element_type=f32)
    carried_ref[...] = carried.reshape(blocks, SLAB, WIDE)

    def one(k, state):
        out_ref[k] = state.astype(bf16)
        return carried_ref[k] * state + pay_ref[k, :, :WIDE].astype(f32)

    lax.fori_loop(0, blocks, one, jnp.zeros((SLAB, WIDE), f32), unroll=8)


def inside_kernel(ahead, place_ref, starts_ref, *refs):
    core = place_ref[0] % CORES
    if ahead:

        @pl.when(core == 0)
        def _():
            inside_terms(True, place_ref, starts_ref, *refs)

    else:
        inside_terms(False, place_ref, starts_ref, *refs)


def inside_terms(
    ahead, place_ref, starts_ref, own_ref, got_ref, x_ref, logit_in, b_in, c_in, gate_in, *refs
):
    base_out, factor_out, logit_ref, b_ref, c_ref, gate_ref, base_ref, factor_ref, spread_ref, sems, sent_sems = refs[-11:]
    place = place_ref[0]
    core = place % CORES
    start = chunk_start(place, starts_ref, core)
    logit_copy = fetch(logit_in, logit_ref, sems.at[0])
    b_copy = fetch(b_in, b_ref, sems.at[1])
    c_copy = fetch(c_in, c_ref, sems.at[2])
    gate_copy = fetch(gate_in, gate_ref, sems.at[3])
    spread_ref[...] = spreader(2 * LANES, 1)
    params = placed([own_ref[i * SLAB : (i + 1) * SLAB] for i in range(HALF)], place, core)
    params = params + placed([got_ref[i * SLAB : (i + 1) * SLAB] for i in range(HALF)], place, 1 - core)
    logit_copy.wait()
    step = softplus(logit_ref[...].astype(f32) + params[0:1])
    p, q = cumulated(step, params[1:2])
    rows = jnp.concatenate([q, p, jnp.broadcast_to(params[2:3], (2 * SLAB, LANES))], axis=0)
    allowed = allowed_pairs(start)
    b_copy.wait()
    c_copy.wait()
    gate_copy.wait()

    def terms(groups):
        sent = []
        for i, (j, half) in enumerate(groups):
            group = CORES * j + half
            columns, states = columns_of(j, half, WIDE), columns_of(j, half, STATE)
            base_ref[group], factor_ref[group] = group_terms(
                rows, group, spread_ref, allowed, x_ref[:, columns], b_ref[:, states], c_ref[:, states], gate_ref[:, columns]
            )
            sent.append(fetch(base_ref.at[group], base_out.at[group], sent_sems.at[0, i]))
            sent.append(fetch(factor_ref.at[group], factor_out.at[group], sent_sems.at[1, i]))
        for copy in sent:
            copy.wait()

    order = [(j, half) for half in (core, 1 - core) for j in range(HALF)]
    if ahead:
        terms(order[:AHEAD])
    else:
        terms(order[AHEAD:])

        @pl.when(core > 0)
        def _():
            terms(order[:AHEAD])


def states_kernel(first_group, place_ref, state_ref, middle_ref, own_ref, sent_ref):
    core = place_ref[0] % CORES
    for i in range(PIECE):
        group = first_group + i
        block = state_ref[:, group].astype(f32)
        first = block.reshape(STATE, WIDE)
        second = (block * middle_ref[group, STATE:][None]).reshape(STATE, WIDE) + middle_ref[group, :STATE]
        own_ref[i] = jnp.where(core == 0, first, second).astype(bf16)
        sent_ref[i] = jnp.where(core == 0, second, first).astype(bf16)


def gated_part(place, starts_ref, half, first_group, base_ref, factor_ref, c_ref, state_ref, gated_ref, power):
    start = chunk_start(place, starts_ref, place % CORES)
    seen = iota((CHUNK, STATE), 0) < start
    for i in range(PIECE):
        group = first_group + i
        of_all = CORES * group + half
        queries = jnp.where(seen, c_ref[:, columns_of(group, half, STATE)].astype(f32), 0.0).astype(bf16)
        outside = jnp.dot(queries, state_ref[i], preferred_element_type=f32)
        gated = base_ref[of_all].astype(f32) + outside * factor_ref[of_all].astype(f32)
        gated_ref[group] = gated
        squares = gated * gated
        for k in range(WIDE // LANES):
            power = power + squares[:, k * LANES : (k + 1) * LANES]
    return power


def own_kernel(place_ref, starts_ref, base_ref, factor_ref, c_ref, *refs):
    *states, gated_ref, power_ref = refs
    place = place_ref[0]
    power = jnp.zeros((CHUNK, LANES), f32)
    for i, state_ref in enumerate(states):
        power = gated_part(
            place, starts_ref, place % CORES, i * PIECE, base_ref, factor_ref, c_ref, state_ref, gated_ref, power
        )
    power_ref[...] = power


def last_kernel(
    place_ref, starts_ref, base_ref, factor_ref, c_ref, *refs
):
    *states, gated_own_ref, power_own_ref, gain_ref, out_ref, gated_ref, done_ref, sems = refs
    place = place_ref[0]
    core = place % CORES
    power = power_own_ref[...]
    for i, state_ref in enumerate(states):
        power = gated_part(
            place, starts_ref, 1 - core, i * PIECE, base_ref, factor_ref, c_ref, state_ref, gated_ref, power
        )
    total = jnp.sum(power, axis=1, keepdims=True)
    scale = lax.rsqrt(total * (1.0 / INNER) + EPS)
    rows = CHUNK // PARTS
    copies = []
    for part in range(PARTS):
        some = slice(part * rows, (part + 1) * rows)
        for half, ref in ((core, gated_own_ref), (1 - core, gated_ref)):
            for group in range(HALF):
                columns = columns_of(group, half, WIDE)
                gated = ref[group, some]
                done_ref[some, columns] = (gated * scale[some] * gain_ref[:, columns]).astype(bf16)
        copies.append(fetch(done_ref.at[some], out_ref.at[some], sems.at[part]))
    for copy in copies:
        copy.wait()


def local(
    head_inputs,
    gate_inputs,
    write_keys,
    read_queries,
    step_logits,
    step_bias,
    decay_log,
    skip_scale,
    norm_gain,
    document_starts,
):
    depth = lax.axis_size("z")
    blocks = lax.axis_size("ctx") * depth
    core = lax.axis_index("core")
    place = (lax.axis_index("z") * CORES + core).astype(jnp.int32).reshape(1)
    swap = [(0, 1), (1, 0)]

    smem = pl.BlockSpec(memory_space=pltpu.SMEM)
    vmem = pl.BlockSpec(memory_space=pltpu.VMEM)

    anywhere = pl.BlockSpec(memory_space=pl.ANY)

    def call(kernel, scalars, operands, out_shape, scratch, name, cost=None, out_specs=None, in_specs=None, mib=24, aliases={}):
        return pl.pallas_call(
            kernel,
            in_specs=[smem] * len(scalars) + (in_specs or [vmem] * len(operands)),
            out_specs=out_specs or [vmem] * len(out_shape),
            out_shape=out_shape,
            scratch_shapes=scratch,
            compiler_params=pltpu.CompilerParams(vmem_limit_bytes=mib * 2**20),
            cost_estimate=cost,
            input_output_aliases=aliases,
            name=name,
        )(*scalars, *operands)

    def shape(dims, kind):
        return jax.ShapeDtypeStruct(dims, kind)

    where = (place, document_starts)

    dma = pltpu.SemaphoreType.DMA
    packed_width = HALF_WIDE + HALF * STATE + LANES
    packed, own, spread_matrix = call(
        pack_kernel,
        (place,),
        (
            *(
                pltpu.with_memory_space_constraint(v, pltpu.HBM)
                for v in (
                    *(v.reshape(1, PER_GROUP) for v in (step_bias, decay_log, skip_scale)),
                    step_logits,
                    head_inputs,
                    write_keys,
                )
            ),
        ),
        [
            pltpu.VMEM((CHUNK, packed_width), bf16),
            pltpu.VMEM((SLAB, LANES), f32),
            pltpu.VMEM((2 * LANES, WIDE), bf16),
        ],
        [pltpu.VMEM((1, PER_GROUP), f32)] * 3 + [dma((2 * HALF + 1,)), dma((3,))],
        "pack",
        in_specs=[anywhere] * 6,
    )
    turns = [own] + [
        lax.ppermute(own, "z", [((i + turn) % depth, i) for i in range(depth)]) for turn in range(1, HALF)
    ]
    packed_got = lax.ppermute(packed, "core", swap)

    own_rows = jnp.concatenate(turns)
    got_rows = lax.ppermute(own_rows, "core", swap)

    def in_hbm(v):
        return pltpu.with_memory_space_constraint(v, pltpu.HBM)

    pay, middle = call(
        write_kernel,
        where,
        (*turns, spread_matrix, step_logits, packed_got, head_inputs, write_keys),
        [
            pltpu.HBM((SLABS, HALF, SLAB, WIDE + LANES), bf16),
            pltpu.HBM((HALF, STATE + SLAB, WIDE), f32),
        ],
        [
            pltpu.VMEM((HALF, SLABS, SLAB, WIDE + LANES), bf16),
            pltpu.VMEM((HALF, STATE + SLAB, WIDE), f32),
            dma((2, HALF)),
        ],
        "write",
        out_specs=[anywhere] * 2,
    )

    def inside(ahead, passed, passed_shapes, name):
        terms = (pltpu.HBM((GROUPS, CHUNK, WIDE), bf16),) * 2
        outs = len(passed_shapes)
        return call(
            functools.partial(inside_kernel, ahead),
            where,
            (
                own_rows,
                got_rows,
                head_inputs,
                *(in_hbm(v) for v in (step_logits, write_keys, read_queries, gate_inputs, *passed)),
            ),
            (*passed_shapes, *terms),
            [
                pltpu.VMEM((CHUNK, LANES), bf16),
                pltpu.VMEM((CHUNK, GROUPS * STATE), bf16),
                pltpu.VMEM((CHUNK, GROUPS * STATE), bf16),
                pltpu.VMEM((CHUNK, INNER), bf16),
                pltpu.VMEM((GROUPS, CHUNK, WIDE), bf16),
                pltpu.VMEM((GROUPS, CHUNK, WIDE), bf16),
                pltpu.VMEM((2 * LANES, WIDE), bf16),
                dma((4,)),
                dma((2, GROUPS)),
            ],
            name,
            pl.CostEstimate(flops=2 * 4 * CHUNK * STATE * INNER, bytes_accessed=9 * 2**20, transcendentals=2**20),
            out_specs=[anywhere] * (outs + 2),
            in_specs=[vmem] * 3 + [anywhere] * (4 + len(passed)),
            aliases={2 + 7 + i: i for i in range(len(passed))},
        )

    pay, base, factor = inside(
        True, (pay,), (pltpu.HBM((SLABS, HALF, SLAB, WIDE + LANES), bf16),), "ahead"
    )
    arrived = lax.all_to_all(
        pay.reshape(blocks, SLAB, WIDE + LANES), ("ctx", "z"), 0, 0, tiled=True
    )
    base, factor = inside(False, (base, factor), (), "inside")
    arrived, base, factor = lax.optimization_barrier((arrived, base, factor))

    [frozen] = call(
        functools.partial(scan_kernel, blocks),
        (),
        (arrived,),
        [shape((blocks, SLAB, WIDE), bf16)],
        [pltpu.VMEM((blocks, SLAB, WIDE), f32)],
        "scan",
    )

    returned = lax.all_to_all(frozen, ("ctx", "z"), 0, 0, tiled=True)

    piece_state = shape((PIECE, STATE, WIDE), bf16)
    states_own, states_sent = [], []
    for first_group in range(0, HALF, PIECE):
        one, other = call(
            functools.partial(states_kernel, first_group),
            (place,),
            (returned.reshape(SLABS, HALF, SLAB, WIDE), middle),
            [piece_state, piece_state],
            [],
            "states",
        )
        states_own.append(one)
        states_sent.append(other)
    states_got = [lax.ppermute(v, "core", swap) for v in states_sent]

    gated, power = call(
        own_kernel,
        where,
        (base, factor, read_queries, *states_own),
        [shape((HALF, CHUNK, WIDE), f32), shape((CHUNK, LANES), f32)],
        [],
        "own",
        pl.CostEstimate(flops=2 * CHUNK * STATE * INNER, bytes_accessed=5 * 2**20, transcendentals=0),
    )

    [out] = call(
        last_kernel,
        where,
        (base, factor, read_queries, *states_got, gated, power, norm_gain.reshape(1, INNER)),
        [shape((CHUNK, INNER), bf16)],
        [
            pltpu.VMEM((HALF, CHUNK, WIDE), f32),
            pltpu.VMEM((CHUNK, INNER), bf16),
            dma((PARTS,)),
        ],
        "last",
        out_specs=[anywhere],
    )
    return out


def solution(mesh):
    ctx, head = mesh.devices.shape
    split = Mesh(mesh.devices.reshape(ctx, head // CORES, CORES), ("ctx", "z", "core"))
    tokens = P(("ctx", "z", "core"), None)
    return jax.shard_map(
        local,
        mesh=split,
        in_specs=(tokens,) * 5 + (P(("z", "core")),) * 3 + (P(), P("ctx")),
        out_specs=tokens,
        check_vma=False,
    )
```

```python
import functools

import jax
import jax.numpy as jnp
from jax import lax
from jax.experimental import pallas as pl
from jax.experimental.pallas import tpu as pltpu
from jax.sharding import Mesh
from jax.sharding import PartitionSpec as P

HEADS = 128
HEAD_DIM = 64
STATE = 128
GROUPS = 8
INNER = HEADS * HEAD_DIM
CHUNK = 128
CORES = 2
HALF = GROUPS // CORES
HALF_HEADS = HEADS // CORES
PER_GROUP = HEADS // GROUPS
WIDE = PER_GROUP * HEAD_DIM
HALF_WIDE = HALF * WIDE
SLAB = 8
SLABS = STATE // SLAB
LANES = 128
PIECE = 4
AHEAD = 5
PARTS = 8
EPS = 1e-5

bf16 = jnp.bfloat16
f32 = jnp.float32


def iota(shape, axis):
    return lax.broadcasted_iota(jnp.int32, shape, axis)


def spreader(rows, parts):
    lane = iota((rows, WIDE), 0) % LANES
    head = iota((rows, WIDE), 1) // HEAD_DIM
    hit = (lane % PER_GROUP == head) & (lane < parts * PER_GROUP)
    return jnp.where(hit, 1.0, 0.0).astype(bf16)


def to_front(v, group):
    return pltpu.roll(v, (2 * LANES - PER_GROUP * group) % LANES, 1)


def spread(v, group, spread_ref):
    front = to_front(v, group)
    high = front.astype(bf16)
    low = (front - high.astype(f32)).astype(bf16)
    return jnp.dot(
        jnp.concatenate([high, low], axis=1), spread_ref[...], preferred_element_type=f32
    )


def from_front(v, group):
    return pltpu.roll(v, PER_GROUP * group, 1)


def columns_of(group, half, width):
    return pl.ds(pl.multiple_of((CORES * group + half) * width, width), width)


def softplus(v):
    return jnp.maximum(v, 0.0) + jnp.log1p(jnp.exp(-jnp.abs(v)))


def cumulated(step, decay):
    rate = -jnp.exp(decay) * step
    lower = iota((CHUNK, 3 * CHUNK), 0) >= iota((CHUNK, 3 * CHUNK), 1) % CHUNK
    parts = []
    for _ in range(3):
        parts.append(rate.astype(bf16))
        rate = rate - parts[-1].astype(f32)
    cum = jnp.dot(
        jnp.where(lower, 1.0, 0.0).astype(bf16), jnp.concatenate(parts, axis=0), preferred_element_type=f32
    )
    return jnp.exp(cum), jnp.exp(-cum) * step


def chunk_start(place, starts_ref, core):
    begun = starts_ref[place // CORES] - core * CHUNK
    return jnp.where((begun >= 0) & (begun < CHUNK), begun, CHUNK)


def fetch(source, target, sem):
    copy = pltpu.make_async_copy(source, target, sem)
    copy.start()
    return copy


def placed(turn_rows, place, core):
    lane = iota((SLAB, LANES), 1)
    params = jnp.zeros((SLAB, LANES), f32)
    for turn, rows in enumerate(turn_rows):
        some = jnp.where(lane < PER_GROUP, rows, 0.0)
        params = params + from_front(some, 2 * ((place // CORES + turn) % HALF) + core)
    return params


def allowed_pairs(start):
    t = iota((CHUNK, CHUNK), 0)
    s = iota((CHUNK, CHUNK), 1)
    return (s <= t) & ((t >= start) == (s >= start))


def group_terms(rows, group, spread_ref, allowed, x, keys, queries, gate):
    wide = spread(rows, group, spread_ref)
    grown = wide[CHUNK : 2 * CHUNK]
    x = x.astype(f32)
    xq = (x * wide[:CHUNK]).astype(bf16)
    score = lax.dot_general(queries, keys, (((1,), (1,)), ((), ())), preferred_element_type=f32)
    mixing = jnp.where(allowed, score, 0.0).astype(bf16)
    inside = jnp.dot(mixing, xq, preferred_element_type=f32)
    skip = wide[2 * CHUNK : 2 * CHUNK + 1]
    gate = gate.astype(f32)
    silu = gate / (1.0 + jnp.exp(-gate))
    return ((inside * grown + skip * x) * silu).astype(bf16), (grown * silu).astype(bf16)


def pack_kernel(
    place_ref, bias_in, decay_in, skip_in, logit_ref, x_ref, b_ref, packed_ref, own_ref, spread_ref,
    bias_ref, decay_ref, skip_ref, sems, row_sems,
):
    core = place_ref[0] % CORES
    tail = HALF_WIDE + HALF * STATE
    rows = [
        fetch(source, target, row_sems.at[i])
        for i, (source, target) in enumerate(
            ((bias_in, bias_ref), (decay_in, decay_ref), (skip_in, skip_ref))
        )
    ]
    copies = [fetch(logit_ref, packed_ref.at[:, pl.ds(tail, LANES)], sems.at[2 * HALF])]
    for group in range(HALF):
        to_x, to_key = pl.ds(group * WIDE, WIDE), pl.ds(HALF_WIDE + group * STATE, STATE)
        copies.append(fetch(x_ref.at[:, columns_of(group, 1 - core, WIDE)], packed_ref.at[:, to_x], sems.at[group]))
        copies.append(
            fetch(b_ref.at[:, columns_of(group, 1 - core, STATE)], packed_ref.at[:, to_key], sems.at[HALF + group])
        )
    spread_ref[...] = spreader(2 * LANES, 1)
    own_ref[...] = jnp.zeros_like(own_ref)
    for i, ref in enumerate((bias_ref, decay_ref, skip_ref)):
        rows[i].wait()
        own_ref[i : i + 1, :PER_GROUP] = ref[...]
    for copy in copies:
        copy.wait()


def write_kernel(
    place_ref, starts_ref, own0, own1, own2, own3, spread_ref, logit_ref, got_ref, x_ref, b_ref,
    pay_out, middle_out, pay_ref, middle_ref, sems,
):
    place = place_ref[0]
    core = place % CORES
    tail = HALF_WIDE + HALF * STATE
    lane = iota((SLAB, LANES), 1)
    params = placed([ref[...] for ref in (own0, own1, own2, own3)], place, core)
    logit = jnp.concatenate([logit_ref[...].astype(f32), got_ref[:, tail:].astype(f32)], axis=1)
    half = iota((CHUNK, 2 * LANES), 1) // PER_GROUP % CORES == core
    both = jnp.concatenate([params, params], axis=1)
    step = jnp.where(half, softplus(logit + both[0:1]), 0.0)
    p, q = cumulated(step, both[1:2])
    last = jnp.broadcast_to(p[CHUNK - 1 : CHUNK], (SLAB, 2 * LANES))
    rows = jnp.concatenate([q[:, :LANES], q[:, LANES:], last[:, :LANES], last[:, LANES:]], axis=0)
    starts = (chunk_start(place, starts_ref, core), chunk_start(place, starts_ref, 1 - core))
    open_ = (starts[0] >= CHUNK, starts[1] >= CHUNK)
    kept = [(iota((CHUNK, STATE), 0) >= start) | (start >= CHUNK) for start in starts]
    whole = jnp.where(open_[0] & open_[1], last[:, :LANES] * last[:, LANES:], 0.0)
    high = whole.astype(bf16).astype(f32)
    middle = (whole - high).astype(bf16).astype(f32)
    low = whole - high - middle

    sent = []
    for j in range(HALF):
        group = 2 * j + core
        columns = slice(j * WIDE, (j + 1) * WIDE)
        at = HALF_WIDE + j * STATE
        xs = (x_ref[:, columns_of(j, core, WIDE)], got_ref[:, columns])
        keys = (b_ref[:, columns_of(j, core, STATE)], got_ref[:, at : at + STATE])
        wide = spread(rows, group, spread_ref)
        lasts = (wide[2 * CHUNK : 2 * CHUNK + SLAB], wide[2 * CHUNK + SLAB :])
        written = []
        for i in range(2):
            xq = (xs[i].astype(f32) * wide[i * CHUNK : (i + 1) * CHUNK]).astype(bf16)
            b = jnp.where(kept[i], keys[i].astype(f32), 0.0).astype(bf16)
            w = lax.dot_general(b, xq, (((0,), (0,)), ((), ())), preferred_element_type=f32)
            written.append(w.reshape(SLABS, SLAB, WIDE) * lasts[i][None])
        decays = [jnp.where(open_[i], lasts[i], 0.0) for i in range(2)]
        second = jnp.where(core == 0, decays[1], decays[0])
        before = jnp.where(core == 0, written[0], written[1])
        after = jnp.where(core == 0, written[1], written[0])
        pay_ref[j, :, :, :WIDE] = (before * second[None] + after).astype(bf16)
        packed = jnp.where(
            lane < PER_GROUP,
            to_front(high, group),
            jnp.where(
                lane < 2 * PER_GROUP,
                to_front(middle, group - 1),
                jnp.where(lane < 3 * PER_GROUP, to_front(low, group - 2), 0.0),
            ),
        ).astype(bf16)
        pay_ref[j, :, :, WIDE:] = jnp.broadcast_to(packed[None], (SLABS, SLAB, LANES))
        sent.append(fetch(pay_ref.at[j], pay_out.at[:, j], sems.at[0, j]))
        middle_ref[j, :STATE] = before.reshape(STATE, WIDE)
        middle_ref[j, STATE:] = jnp.where(core == 0, decays[0], decays[1])
        sent.append(fetch(middle_ref.at[j], middle_out.at[j], sems.at[1, j]))
    for copy in sent:
        copy.wait()


def scan_kernel(blocks, pay_ref, out_ref, carried_ref):
    packed = pay_ref[:, :, WIDE:].astype(f32).reshape(blocks * SLAB, LANES).astype(bf16)
    carried = jnp.dot(packed, spreader(LANES, 3), preferred_element_type=f32)
    carried_ref[...] = carried.reshape(blocks, SLAB, WIDE)

    def one(k, state):
        out_ref[k] = state.astype(bf16)
        return carried_ref[k] * state + pay_ref[k, :, :WIDE].astype(f32)

    lax.fori_loop(0, blocks, one, jnp.zeros((SLAB, WIDE), f32), unroll=8)


def inside_kernel(ahead, place_ref, starts_ref, *refs):
    core = place_ref[0] % CORES
    if ahead:

        @pl.when(core == 0)
        def _():
            inside_terms(True, place_ref, starts_ref, *refs)

    else:
        inside_terms(False, place_ref, starts_ref, *refs)


def inside_terms(
    ahead, place_ref, starts_ref, own_ref, got_ref, x_ref, logit_in, b_in, c_in, gate_in, *refs
):
    base_out, factor_out, logit_ref, b_ref, c_ref, gate_ref, base_ref, factor_ref, spread_ref, sems, sent_sems = refs[-11:]
    place = place_ref[0]
    core = place % CORES
    start = chunk_start(place, starts_ref, core)
    logit_copy = fetch(logit_in, logit_ref, sems.at[0])
    b_copy = fetch(b_in, b_ref, sems.at[1])
    c_copy = fetch(c_in, c_ref, sems.at[2])
    gate_copy = fetch(gate_in, gate_ref, sems.at[3])
    spread_ref[...] = spreader(2 * LANES, 1)
    params = placed([own_ref[i * SLAB : (i + 1) * SLAB] for i in range(HALF)], place, core)
    params = params + placed([got_ref[i * SLAB : (i + 1) * SLAB] for i in range(HALF)], place, 1 - core)
    logit_copy.wait()
    step = softplus(logit_ref[...].astype(f32) + params[0:1])
    p, q = cumulated(step, params[1:2])
    rows = jnp.concatenate([q, p, jnp.broadcast_to(params[2:3], (2 * SLAB, LANES))], axis=0)
    allowed = allowed_pairs(start)
    b_copy.wait()
    c_copy.wait()
    gate_copy.wait()

    def terms(groups):
        sent = []
        for i, (j, half) in enumerate(groups):
            group = CORES * j + half
            columns, states = columns_of(j, half, WIDE), columns_of(j, half, STATE)
            base_ref[group], factor_ref[group] = group_terms(
                rows, group, spread_ref, allowed, x_ref[:, columns], b_ref[:, states], c_ref[:, states], gate_ref[:, columns]
            )
            sent.append(fetch(base_ref.at[group], base_out.at[group], sent_sems.at[0, i]))
            sent.append(fetch(factor_ref.at[group], factor_out.at[group], sent_sems.at[1, i]))
        for copy in sent:
            copy.wait()

    order = [(j, half) for half in (core, 1 - core) for j in range(HALF)]
    if ahead:
        terms(order[:AHEAD])
    else:
        terms(order[AHEAD:])

        @pl.when(core > 0)
        def _():
            terms(order[:AHEAD])


def states_kernel(first_group, place_ref, state_ref, middle_ref, own_ref, sent_ref):
    core = place_ref[0] % CORES
    for i in range(PIECE):
        group = first_group + i
        block = state_ref[:, group].astype(f32)
        first = block.reshape(STATE, WIDE)
        second = (block * middle_ref[group, STATE:][None]).reshape(STATE, WIDE) + middle_ref[group, :STATE]
        own_ref[i] = jnp.where(core == 0, first, second).astype(bf16)
        sent_ref[i] = jnp.where(core == 0, second, first).astype(bf16)


def gated_part(place, starts_ref, half, first_group, base_ref, factor_ref, c_ref, state_ref, gain_ref, gated_ref, power):
    start = chunk_start(place, starts_ref, place % CORES)
    seen = iota((CHUNK, STATE), 0) < start
    for i in range(PIECE):
        group = first_group + i
        of_all = CORES * group + half
        queries = jnp.where(seen, c_ref[:, columns_of(group, half, STATE)].astype(f32), 0.0).astype(bf16)
        outside = jnp.dot(queries, state_ref[i], preferred_element_type=f32)
        gated = base_ref[of_all].astype(f32) + outside * factor_ref[of_all].astype(f32)
        gated_ref[group] = gated * gain_ref[:, columns_of(group, half, WIDE)]
        squares = gated * gated
        for k in range(WIDE // LANES):
            power = power + squares[:, k * LANES : (k + 1) * LANES]
    return power


def own_kernel(place_ref, starts_ref, base_ref, factor_ref, c_ref, gain_ref, *refs):
    *states, gated_ref, power_ref = refs
    place = place_ref[0]
    power = jnp.zeros((CHUNK, LANES), f32)
    for i, state_ref in enumerate(states):
        power = gated_part(
            place, starts_ref, place % CORES, i * PIECE, base_ref, factor_ref, c_ref, state_ref, gain_ref, gated_ref, power
        )
    power_ref[...] = power


def last_kernel(
    place_ref, starts_ref, base_ref, factor_ref, c_ref, *refs
):
    *states, gated_own_ref, power_own_ref, gain_ref, out_ref, gated_ref, done_ref, sems = refs
    place = place_ref[0]
    core = place % CORES
    power = power_own_ref[...]
    for i, state_ref in enumerate(states):
        power = gated_part(
            place, starts_ref, 1 - core, i * PIECE, base_ref, factor_ref, c_ref, state_ref, gain_ref, gated_ref, power
        )
    total = jnp.sum(power, axis=1, keepdims=True)
    scale = lax.rsqrt(total * (1.0 / INNER) + EPS)
    rows = CHUNK // PARTS
    copies = []
    for part in range(PARTS):
        some = slice(part * rows, (part + 1) * rows)
        wide_scale = jnp.broadcast_to(scale[some], (rows, WIDE))
        for half, ref in ((core, gated_own_ref), (1 - core, gated_ref)):
            for group in range(HALF):
                columns = columns_of(group, half, WIDE)
                gated = ref[group, some]
                done_ref[some, columns] = (gated * wide_scale).astype(bf16)
        copies.append(fetch(done_ref.at[some], out_ref.at[some], sems.at[part]))
    for copy in copies:
        copy.wait()


def local(
    head_inputs,
    gate_inputs,
    write_keys,
    read_queries,
    step_logits,
    step_bias,
    decay_log,
    skip_scale,
    norm_gain,
    document_starts,
):
    depth = lax.axis_size("z")
    blocks = lax.axis_size("ctx") * depth
    core = lax.axis_index("core")
    place = (lax.axis_index("z") * CORES + core).astype(jnp.int32).reshape(1)
    swap = [(0, 1), (1, 0)]

    smem = pl.BlockSpec(memory_space=pltpu.SMEM)
    vmem = pl.BlockSpec(memory_space=pltpu.VMEM)

    anywhere = pl.BlockSpec(memory_space=pl.ANY)

    def call(kernel, scalars, operands, out_shape, scratch, name, cost=None, out_specs=None, in_specs=None, mib=24, aliases={}):
        return pl.pallas_call(
            kernel,
            in_specs=[smem] * len(scalars) + (in_specs or [vmem] * len(operands)),
            out_specs=out_specs or [vmem] * len(out_shape),
            out_shape=out_shape,
            scratch_shapes=scratch,
            compiler_params=pltpu.CompilerParams(vmem_limit_bytes=mib * 2**20),
            cost_estimate=cost,
            input_output_aliases=aliases,
            name=name,
        )(*scalars, *operands)

    def shape(dims, kind):
        return jax.ShapeDtypeStruct(dims, kind)

    where = (place, document_starts)

    dma = pltpu.SemaphoreType.DMA
    packed_width = HALF_WIDE + HALF * STATE + LANES
    packed, own, spread_matrix = call(
        pack_kernel,
        (place,),
        (
            *(
                pltpu.with_memory_space_constraint(v, pltpu.HBM)
                for v in (
                    *(v.reshape(1, PER_GROUP) for v in (step_bias, decay_log, skip_scale)),
                    step_logits,
                    head_inputs,
                    write_keys,
                )
            ),
        ),
        [
            pltpu.VMEM((CHUNK, packed_width), bf16),
            pltpu.VMEM((SLAB, LANES), f32),
            pltpu.VMEM((2 * LANES, WIDE), bf16),
        ],
        [pltpu.VMEM((1, PER_GROUP), f32)] * 3 + [dma((2 * HALF + 1,)), dma((3,))],
        "pack",
        in_specs=[anywhere] * 6,
    )
    turns = [own] + [
        lax.ppermute(own, "z", [((i + turn) % depth, i) for i in range(depth)]) for turn in range(1, HALF)
    ]
    packed_got = lax.ppermute(packed, "core", swap)

    own_rows = jnp.concatenate(turns)
    got_rows = lax.ppermute(own_rows, "core", swap)

    def in_hbm(v):
        return pltpu.with_memory_space_constraint(v, pltpu.HBM)

    pay, middle = call(
        write_kernel,
        where,
        (*turns, spread_matrix, step_logits, packed_got, head_inputs, write_keys),
        [
            pltpu.HBM((SLABS, HALF, SLAB, WIDE + LANES), bf16),
            pltpu.HBM((HALF, STATE + SLAB, WIDE), f32),
        ],
        [
            pltpu.VMEM((HALF, SLABS, SLAB, WIDE + LANES), bf16),
            pltpu.VMEM((HALF, STATE + SLAB, WIDE), f32),
            dma((2, HALF)),
        ],
        "write",
        out_specs=[anywhere] * 2,
    )

    def inside(ahead, passed, passed_shapes, name):
        terms = (pltpu.HBM((GROUPS, CHUNK, WIDE), bf16),) * 2
        outs = len(passed_shapes)
        return call(
            functools.partial(inside_kernel, ahead),
            where,
            (
                own_rows,
                got_rows,
                head_inputs,
                *(in_hbm(v) for v in (step_logits, write_keys, read_queries, gate_inputs, *passed)),
            ),
            (*passed_shapes, *terms),
            [
                pltpu.VMEM((CHUNK, LANES), bf16),
                pltpu.VMEM((CHUNK, GROUPS * STATE), bf16),
                pltpu.VMEM((CHUNK, GROUPS * STATE), bf16),
                pltpu.VMEM((CHUNK, INNER), bf16),
                pltpu.VMEM((GROUPS, CHUNK, WIDE), bf16),
                pltpu.VMEM((GROUPS, CHUNK, WIDE), bf16),
                pltpu.VMEM((2 * LANES, WIDE), bf16),
                dma((4,)),
                dma((2, GROUPS)),
            ],
            name,
            pl.CostEstimate(flops=2 * 4 * CHUNK * STATE * INNER, bytes_accessed=9 * 2**20, transcendentals=2**20),
            out_specs=[anywhere] * (outs + 2),
            in_specs=[vmem] * 3 + [anywhere] * (4 + len(passed)),
            aliases={2 + 7 + i: i for i in range(len(passed))},
        )

    pay, base, factor = inside(
        True, (pay,), (pltpu.HBM((SLABS, HALF, SLAB, WIDE + LANES), bf16),), "ahead"
    )
    arrived = lax.all_to_all(
        pay.reshape(blocks, SLAB, WIDE + LANES), ("ctx", "z"), 0, 0, tiled=True
    )
    base, factor = inside(False, (base, factor), (), "inside")
    arrived, base, factor = lax.optimization_barrier((arrived, base, factor))

    [frozen] = call(
        functools.partial(scan_kernel, blocks),
        (),
        (arrived,),
        [shape((blocks, SLAB, WIDE), bf16)],
        [pltpu.VMEM((blocks, SLAB, WIDE), f32)],
        "scan",
    )

    returned = lax.all_to_all(frozen, ("ctx", "z"), 0, 0, tiled=True)

    piece_state = shape((PIECE, STATE, WIDE), bf16)
    states_own, states_sent = [], []
    for first_group in range(0, HALF, PIECE):
        one, other = call(
            functools.partial(states_kernel, first_group),
            (place,),
            (returned.reshape(SLABS, HALF, SLAB, WIDE), middle),
            [piece_state, piece_state],
            [],
            "states",
        )
        states_own.append(one)
        states_sent.append(other)
    states_got = [lax.ppermute(v, "core", swap) for v in states_sent]

    gated, power = call(
        own_kernel,
        where,
        (base, factor, read_queries, norm_gain.reshape(1, INNER), *states_own),
        [shape((HALF, CHUNK, WIDE), f32), shape((CHUNK, LANES), f32)],
        [],
        "own",
        pl.CostEstimate(flops=2 * CHUNK * STATE * INNER, bytes_accessed=5 * 2**20, transcendentals=0),
    )

    [out] = call(
        last_kernel,
        where,
        (base, factor, read_queries, *states_got, gated, power, norm_gain.reshape(1, INNER)),
        [shape((CHUNK, INNER), bf16)],
        [
            pltpu.VMEM((HALF, CHUNK, WIDE), f32),
            pltpu.VMEM((CHUNK, INNER), bf16),
            dma((PARTS,)),
        ],
        "last",
        out_specs=[anywhere],
    )
    return out


def solution(mesh):
    ctx, head = mesh.devices.shape
    split = Mesh(mesh.devices.reshape(ctx, head // CORES, CORES), ("ctx", "z", "core"))
    tokens = P(("ctx", "z", "core"), None)
    return jax.shard_map(
        local,
        mesh=split,
        in_specs=(tokens,) * 5 + (P(("z", "core")),) * 3 + (P(), P("ctx")),
        out_specs=tokens,
        check_vma=False,
    )
```

```python
import functools

import jax
import jax.numpy as jnp
from jax import lax
from jax.experimental import pallas as pl
from jax.experimental.pallas import tpu as pltpu
from jax.sharding import Mesh
from jax.sharding import PartitionSpec as P

HEADS = 128
HEAD_DIM = 64
STATE = 128
GROUPS = 8
INNER = HEADS * HEAD_DIM
CHUNK = 128
CORES = 2
HALF = GROUPS // CORES
HALF_HEADS = HEADS // CORES
PER_GROUP = HEADS // GROUPS
WIDE = PER_GROUP * HEAD_DIM
HALF_WIDE = HALF * WIDE
SLAB = 8
SLABS = STATE // SLAB
LANES = 128
PIECE = 4
AHEAD = 6
PARTS = 8
EPS = 1e-5

bf16 = jnp.bfloat16
f32 = jnp.float32


def iota(shape, axis):
    return lax.broadcasted_iota(jnp.int32, shape, axis)


def spreader(rows, parts):
    lane = iota((rows, WIDE), 0) % LANES
    head = iota((rows, WIDE), 1) // HEAD_DIM
    hit = (lane % PER_GROUP == head) & (lane < parts * PER_GROUP)
    return jnp.where(hit, 1.0, 0.0).astype(bf16)


def to_front(v, group):
    return pltpu.roll(v, (2 * LANES - PER_GROUP * group) % LANES, 1)


def spread(v, group, spread_ref):
    front = to_front(v, group)
    high = front.astype(bf16)
    low = (front - high.astype(f32)).astype(bf16)
    return jnp.dot(
        jnp.concatenate([high, low], axis=1), spread_ref[...], preferred_element_type=f32
    )


def from_front(v, group):
    return pltpu.roll(v, PER_GROUP * group, 1)


def columns_of(group, half, width):
    return pl.ds(pl.multiple_of((CORES * group + half) * width, width), width)


def softplus(v):
    return jnp.maximum(v, 0.0) + jnp.log1p(jnp.exp(-jnp.abs(v)))


def cumulated(step, decay):
    rate = -jnp.exp(decay) * step
    lower = iota((CHUNK, 3 * CHUNK), 0) >= iota((CHUNK, 3 * CHUNK), 1) % CHUNK
    parts = []
    for _ in range(3):
        parts.append(rate.astype(bf16))
        rate = rate - parts[-1].astype(f32)
    cum = jnp.dot(
        jnp.where(lower, 1.0, 0.0).astype(bf16), jnp.concatenate(parts, axis=0), preferred_element_type=f32
    )
    return jnp.exp(cum), jnp.exp(-cum) * step


def chunk_start(place, starts_ref, core):
    begun = starts_ref[place // CORES] - core * CHUNK
    return jnp.where((begun >= 0) & (begun < CHUNK), begun, CHUNK)


def fetch(source, target, sem):
    copy = pltpu.make_async_copy(source, target, sem)
    copy.start()
    return copy


def placed(turn_rows, place, core):
    lane = iota((SLAB, LANES), 1)
    params = jnp.zeros((SLAB, LANES), f32)
    for turn, rows in enumerate(turn_rows):
        some = jnp.where(lane < PER_GROUP, rows, 0.0)
        params = params + from_front(some, 2 * ((place // CORES + turn) % HALF) + core)
    return params


def allowed_pairs(start):
    t = iota((CHUNK, CHUNK), 0)
    s = iota((CHUNK, CHUNK), 1)
    return (s <= t) & ((t >= start) == (s >= start))


def group_terms(rows, group, spread_ref, allowed, x, keys, queries, gate):
    wide = spread(rows, group, spread_ref)
    grown = wide[CHUNK : 2 * CHUNK]
    x = x.astype(f32)
    xq = (x * wide[:CHUNK]).astype(bf16)
    score = lax.dot_general(queries, keys, (((1,), (1,)), ((), ())), preferred_element_type=f32)
    mixing = jnp.where(allowed, score, 0.0).astype(bf16)
    inside = jnp.dot(mixing, xq, preferred_element_type=f32)
    skip = wide[2 * CHUNK : 2 * CHUNK + 1]
    gate = gate.astype(f32)
    silu = gate / (1.0 + jnp.exp(-gate))
    return ((inside * grown + skip * x) * silu).astype(bf16), (grown * silu).astype(bf16)


def pack_kernel(
    place_ref, bias_in, decay_in, skip_in, logit_ref, x_ref, b_ref, packed_ref, own_ref, spread_ref,
    bias_ref, decay_ref, skip_ref, sems, row_sems,
):
    core = place_ref[0] % CORES
    tail = HALF_WIDE + HALF * STATE
    rows = [
        fetch(source, target, row_sems.at[i])
        for i, (source, target) in enumerate(
            ((bias_in, bias_ref), (decay_in, decay_ref), (skip_in, skip_ref))
        )
    ]
    copies = [fetch(logit_ref, packed_ref.at[:, pl.ds(tail, LANES)], sems.at[2 * HALF])]
    for group in range(HALF):
        to_x, to_key = pl.ds(group * WIDE, WIDE), pl.ds(HALF_WIDE + group * STATE, STATE)
        copies.append(fetch(x_ref.at[:, columns_of(group, 1 - core, WIDE)], packed_ref.at[:, to_x], sems.at[group]))
        copies.append(
            fetch(b_ref.at[:, columns_of(group, 1 - core, STATE)], packed_ref.at[:, to_key], sems.at[HALF + group])
        )
    spread_ref[...] = spreader(2 * LANES, 1)
    own_ref[...] = jnp.zeros_like(own_ref)
    for i, ref in enumerate((bias_ref, decay_ref, skip_ref)):
        rows[i].wait()
        own_ref[i : i + 1, :PER_GROUP] = ref[...]
    for copy in copies:
        copy.wait()


def write_kernel(
    place_ref, starts_ref, own0, own1, own2, own3, spread_ref, logit_ref, got_ref, x_ref, b_ref,
    pay_out, middle_out, pay_ref, middle_ref, sems,
):
    place = place_ref[0]
    core = place % CORES
    tail = HALF_WIDE + HALF * STATE
    lane = iota((SLAB, LANES), 1)
    params = placed([ref[...] for ref in (own0, own1, own2, own3)], place, core)
    logit = jnp.concatenate([logit_ref[...].astype(f32), got_ref[:, tail:].astype(f32)], axis=1)
    half = iota((CHUNK, 2 * LANES), 1) // PER_GROUP % CORES == core
    both = jnp.concatenate([params, params], axis=1)
    step = jnp.where(half, softplus(logit + both[0:1]), 0.0)
    p, q = cumulated(step, both[1:2])
    last = jnp.broadcast_to(p[CHUNK - 1 : CHUNK], (SLAB, 2 * LANES))
    rows = jnp.concatenate([q[:, :LANES], q[:, LANES:], last[:, :LANES], last[:, LANES:]], axis=0)
    starts = (chunk_start(place, starts_ref, core), chunk_start(place, starts_ref, 1 - core))
    open_ = (starts[0] >= CHUNK, starts[1] >= CHUNK)
    kept = [(iota((CHUNK, STATE), 0) >= start) | (start >= CHUNK) for start in starts]
    whole = jnp.where(open_[0] & open_[1], last[:, :LANES] * last[:, LANES:], 0.0)
    high = whole.astype(bf16).astype(f32)
    middle = (whole - high).astype(bf16).astype(f32)
    low = whole - high - middle

    sent = []
    for j in range(HALF):
        group = 2 * j + core
        columns = slice(j * WIDE, (j + 1) * WIDE)
        at = HALF_WIDE + j * STATE
        xs = (x_ref[:, columns_of(j, core, WIDE)], got_ref[:, columns])
        keys = (b_ref[:, columns_of(j, core, STATE)], got_ref[:, at : at + STATE])
        wide = spread(rows, group, spread_ref)
        lasts = (wide[2 * CHUNK : 2 * CHUNK + SLAB], wide[2 * CHUNK + SLAB :])
        written = []
        for i in range(2):
            xq = (xs[i].astype(f32) * wide[i * CHUNK : (i + 1) * CHUNK]).astype(bf16)
            b = jnp.where(kept[i], keys[i].astype(f32), 0.0).astype(bf16)
            w = lax.dot_general(b, xq, (((0,), (0,)), ((), ())), preferred_element_type=f32)
            written.append(w.reshape(SLABS, SLAB, WIDE) * lasts[i][None])
        decays = [jnp.where(open_[i], lasts[i], 0.0) for i in range(2)]
        second = jnp.where(core == 0, decays[1], decays[0])
        before = jnp.where(core == 0, written[0], written[1])
        after = jnp.where(core == 0, written[1], written[0])
        pay_ref[j, :, :, :WIDE] = (before * second[None] + after).astype(bf16)
        packed = jnp.where(
            lane < PER_GROUP,
            to_front(high, group),
            jnp.where(
                lane < 2 * PER_GROUP,
                to_front(middle, group - 1),
                jnp.where(lane < 3 * PER_GROUP, to_front(low, group - 2), 0.0),
            ),
        ).astype(bf16)
        pay_ref[j, :, :, WIDE:] = jnp.broadcast_to(packed[None], (SLABS, SLAB, LANES))
        sent.append(fetch(pay_ref.at[j], pay_out.at[:, j], sems.at[0, j]))
        middle_ref[j, :STATE] = before.reshape(STATE, WIDE)
        middle_ref[j, STATE:] = jnp.where(core == 0, decays[0], decays[1])
        sent.append(fetch(middle_ref.at[j], middle_out.at[j], sems.at[1, j]))
    for copy in sent:
        copy.wait()


def scan_kernel(blocks, pay_ref, out_ref, carried_ref):
    packed = pay_ref[:, :, WIDE:].astype(f32).reshape(blocks * SLAB, LANES).astype(bf16)
    carried = jnp.dot(packed, spreader(LANES, 3), preferred_element_type=f32)
    carried_ref[...] = carried.reshape(blocks, SLAB, WIDE)

    def one(k, state):
        out_ref[k] = state.astype(bf16)
        return carried_ref[k] * state + pay_ref[k, :, :WIDE].astype(f32)

    lax.fori_loop(0, blocks, one, jnp.zeros((SLAB, WIDE), f32), unroll=8)


def inside_kernel(ahead, place_ref, starts_ref, *refs):
    core = place_ref[0] % CORES
    if ahead:

        @pl.when(core == 0)
        def _():
            inside_terms(True, place_ref, starts_ref, *refs)

    else:
        inside_terms(False, place_ref, starts_ref, *refs)


def inside_terms(
    ahead, place_ref, starts_ref, own_ref, got_ref, x_ref, logit_in, b_in, c_in, gate_in, *refs
):
    base_out, factor_out, logit_ref, b_ref, c_ref, gate_ref, base_ref, factor_ref, spread_ref, sems, sent_sems = refs[-11:]
    place = place_ref[0]
    core = place % CORES
    start = chunk_start(place, starts_ref, core)
    logit_copy = fetch(logit_in, logit_ref, sems.at[0])
    b_copy = fetch(b_in, b_ref, sems.at[1])
    c_copy = fetch(c_in, c_ref, sems.at[2])
    gate_copy = fetch(gate_in, gate_ref, sems.at[3])
    spread_ref[...] = spreader(2 * LANES, 1)
    params = placed([own_ref[i * SLAB : (i + 1) * SLAB] for i in range(HALF)], place, core)
    params = params + placed([got_ref[i * SLAB : (i + 1) * SLAB] for i in range(HALF)], place, 1 - core)
    logit_copy.wait()
    step = softplus(logit_ref[...].astype(f32) + params[0:1])
    p, q = cumulated(step, params[1:2])
    rows = jnp.concatenate([q, p, jnp.broadcast_to(params[2:3], (2 * SLAB, LANES))], axis=0)
    allowed = allowed_pairs(start)
    b_copy.wait()
    c_copy.wait()
    gate_copy.wait()

    def terms(groups):
        sent = []
        for i, (j, half) in enumerate(groups):
            group = CORES * j + half
            columns, states = columns_of(j, half, WIDE), columns_of(j, half, STATE)
            base_ref[group], factor_ref[group] = group_terms(
                rows, group, spread_ref, allowed, x_ref[:, columns], b_ref[:, states], c_ref[:, states], gate_ref[:, columns]
            )
            sent.append(fetch(base_ref.at[group], base_out.at[group], sent_sems.at[0, i]))
            sent.append(fetch(factor_ref.at[group], factor_out.at[group], sent_sems.at[1, i]))
        for copy in sent:
            copy.wait()

    order = [(j, half) for half in (core, 1 - core) for j in range(HALF)]
    if ahead:
        terms(order[:AHEAD])
    else:
        terms(order[AHEAD:])

        @pl.when(core > 0)
        def _():
            terms(order[:AHEAD])


def states_kernel(first_group, place_ref, state_ref, middle_ref, own_ref, sent_ref):
    core = place_ref[0] % CORES
    for i in range(PIECE):
        group = first_group + i
        block = state_ref[:, group].astype(f32)
        first = block.reshape(STATE, WIDE)
        second = (block * middle_ref[group, STATE:][None]).reshape(STATE, WIDE) + middle_ref[group, :STATE]
        own_ref[i] = jnp.where(core == 0, first, second).astype(bf16)
        sent_ref[i] = jnp.where(core == 0, second, first).astype(bf16)


def gated_part(place, starts_ref, half, first_group, base_ref, factor_ref, c_ref, state_ref, gain_ref, gated_ref, power):
    start = chunk_start(place, starts_ref, place % CORES)
    seen = iota((CHUNK, STATE), 0) < start
    for i in range(PIECE):
        group = first_group + i
        of_all = CORES * group + half
        queries = jnp.where(seen, c_ref[:, columns_of(group, half, STATE)].astype(f32), 0.0).astype(bf16)
        outside = jnp.dot(queries, state_ref[i], preferred_element_type=f32)
        gated = base_ref[of_all].astype(f32) + outside * factor_ref[of_all].astype(f32)
        gated_ref[group] = gated * gain_ref[:, columns_of(group, half, WIDE)]
        squares = gated * gated
        for k in range(WIDE // LANES):
            power = power + squares[:, k * LANES : (k + 1) * LANES]
    return power


def own_kernel(place_ref, starts_ref, base_ref, factor_ref, c_ref, gain_ref, *refs):
    *states, gated_ref, power_ref = refs
    place = place_ref[0]
    power = jnp.zeros((CHUNK, LANES), f32)
    for i, state_ref in enumerate(states):
        power = gated_part(
            place, starts_ref, place % CORES, i * PIECE, base_ref, factor_ref, c_ref, state_ref, gain_ref, gated_ref, power
        )
    power_ref[...] = power


def last_kernel(
    place_ref, starts_ref, base_ref, factor_ref, c_ref, *refs
):
    *states, gated_own_ref, power_own_ref, gain_ref, out_ref, gated_ref, done_ref, sems = refs
    place = place_ref[0]
    core = place % CORES
    power = power_own_ref[...]
    for i, state_ref in enumerate(states):
        power = gated_part(
            place, starts_ref, 1 - core, i * PIECE, base_ref, factor_ref, c_ref, state_ref, gain_ref, gated_ref, power
        )
    total = jnp.sum(power, axis=1, keepdims=True)
    scale = lax.rsqrt(total * (1.0 / INNER) + EPS)
    rows = CHUNK // PARTS
    copies = []
    for part in range(PARTS):
        some = slice(part * rows, (part + 1) * rows)
        wide_scale = jnp.broadcast_to(scale[some], (rows, WIDE))
        for half, ref in ((core, gated_own_ref), (1 - core, gated_ref)):
            for group in range(HALF):
                columns = columns_of(group, half, WIDE)
                gated = ref[group, some]
                done_ref[some, columns] = (gated * wide_scale).astype(bf16)
        copies.append(fetch(done_ref.at[some], out_ref.at[some], sems.at[part]))
    for copy in copies:
        copy.wait()


def local(
    head_inputs,
    gate_inputs,
    write_keys,
    read_queries,
    step_logits,
    step_bias,
    decay_log,
    skip_scale,
    norm_gain,
    document_starts,
):
    depth = lax.axis_size("z")
    blocks = lax.axis_size("ctx") * depth
    core = lax.axis_index("core")
    place = (lax.axis_index("z") * CORES + core).astype(jnp.int32).reshape(1)
    swap = [(0, 1), (1, 0)]

    smem = pl.BlockSpec(memory_space=pltpu.SMEM)
    vmem = pl.BlockSpec(memory_space=pltpu.VMEM)

    anywhere = pl.BlockSpec(memory_space=pl.ANY)

    def call(kernel, scalars, operands, out_shape, scratch, name, cost=None, out_specs=None, in_specs=None, mib=24, aliases={}):
        return pl.pallas_call(
            kernel,
            in_specs=[smem] * len(scalars) + (in_specs or [vmem] * len(operands)),
            out_specs=out_specs or [vmem] * len(out_shape),
            out_shape=out_shape,
            scratch_shapes=scratch,
            compiler_params=pltpu.CompilerParams(vmem_limit_bytes=mib * 2**20),
            cost_estimate=cost,
            input_output_aliases=aliases,
            name=name,
        )(*scalars, *operands)

    def shape(dims, kind):
        return jax.ShapeDtypeStruct(dims, kind)

    where = (place, document_starts)

    dma = pltpu.SemaphoreType.DMA
    packed_width = HALF_WIDE + HALF * STATE + LANES
    packed, own, spread_matrix = call(
        pack_kernel,
        (place,),
        (
            *(
                pltpu.with_memory_space_constraint(v, pltpu.HBM)
                for v in (
                    *(v.reshape(1, PER_GROUP) for v in (step_bias, decay_log, skip_scale)),
                    step_logits,
                    head_inputs,
                    write_keys,
                )
            ),
        ),
        [
            pltpu.VMEM((CHUNK, packed_width), bf16),
            pltpu.VMEM((SLAB, LANES), f32),
            pltpu.VMEM((2 * LANES, WIDE), bf16),
        ],
        [pltpu.VMEM((1, PER_GROUP), f32)] * 3 + [dma((2 * HALF + 1,)), dma((3,))],
        "pack",
        in_specs=[anywhere] * 6,
    )
    turns = [own] + [
        lax.ppermute(own, "z", [((i + turn) % depth, i) for i in range(depth)]) for turn in range(1, HALF)
    ]
    packed_got = lax.ppermute(packed, "core", swap)

    own_rows = jnp.concatenate(turns)
    got_rows = lax.ppermute(own_rows, "core", swap)

    def in_hbm(v):
        return pltpu.with_memory_space_constraint(v, pltpu.HBM)

    pay, middle = call(
        write_kernel,
        where,
        (*turns, spread_matrix, step_logits, packed_got, head_inputs, write_keys),
        [
            pltpu.HBM((SLABS, HALF, SLAB, WIDE + LANES), bf16),
            pltpu.HBM((HALF, STATE + SLAB, WIDE), f32),
        ],
        [
            pltpu.VMEM((HALF, SLABS, SLAB, WIDE + LANES), bf16),
            pltpu.VMEM((HALF, STATE + SLAB, WIDE), f32),
            dma((2, HALF)),
        ],
        "write",
        out_specs=[anywhere] * 2,
    )

    def inside(ahead, passed, passed_shapes, name):
        terms = (pltpu.HBM((GROUPS, CHUNK, WIDE), bf16),) * 2
        outs = len(passed_shapes)
        return call(
            functools.partial(inside_kernel, ahead),
            where,
            (
                own_rows,
                got_rows,
                head_inputs,
                *(in_hbm(v) for v in (step_logits, write_keys, read_queries, gate_inputs, *passed)),
            ),
            (*passed_shapes, *terms),
            [
                pltpu.VMEM((CHUNK, LANES), bf16),
                pltpu.VMEM((CHUNK, GROUPS * STATE), bf16),
                pltpu.VMEM((CHUNK, GROUPS * STATE), bf16),
                pltpu.VMEM((CHUNK, INNER), bf16),
                pltpu.VMEM((GROUPS, CHUNK, WIDE), bf16),
                pltpu.VMEM((GROUPS, CHUNK, WIDE), bf16),
                pltpu.VMEM((2 * LANES, WIDE), bf16),
                dma((4,)),
                dma((2, GROUPS)),
            ],
            name,
            pl.CostEstimate(flops=2 * 4 * CHUNK * STATE * INNER, bytes_accessed=9 * 2**20, transcendentals=2**20),
            out_specs=[anywhere] * (outs + 2),
            in_specs=[vmem] * 3 + [anywhere] * (4 + len(passed)),
            aliases={2 + 7 + i: i for i in range(len(passed))},
        )

    pay, base, factor = inside(
        True, (pay,), (pltpu.HBM((SLABS, HALF, SLAB, WIDE + LANES), bf16),), "ahead"
    )
    arrived = lax.all_to_all(
        pay.reshape(blocks, SLAB, WIDE + LANES), ("ctx", "z"), 0, 0, tiled=True
    )
    base, factor = inside(False, (base, factor), (), "inside")
    arrived, base, factor = lax.optimization_barrier((arrived, base, factor))

    [frozen] = call(
        functools.partial(scan_kernel, blocks),
        (),
        (arrived,),
        [shape((blocks, SLAB, WIDE), bf16)],
        [pltpu.VMEM((blocks, SLAB, WIDE), f32)],
        "scan",
    )

    returned = lax.all_to_all(frozen, ("ctx", "z"), 0, 0, tiled=True)

    piece_state = shape((PIECE, STATE, WIDE), bf16)
    states_own, states_sent = [], []
    for first_group in range(0, HALF, PIECE):
        one, other = call(
            functools.partial(states_kernel, first_group),
            (place,),
            (returned.reshape(SLABS, HALF, SLAB, WIDE), middle),
            [piece_state, piece_state],
            [],
            "states",
        )
        states_own.append(one)
        states_sent.append(other)
    states_got = [lax.ppermute(v, "core", swap) for v in states_sent]

    gated, power = call(
        own_kernel,
        where,
        (base, factor, read_queries, norm_gain.reshape(1, INNER), *states_own),
        [shape((HALF, CHUNK, WIDE), f32), shape((CHUNK, LANES), f32)],
        [],
        "own",
        pl.CostEstimate(flops=2 * CHUNK * STATE * INNER, bytes_accessed=5 * 2**20, transcendentals=0),
    )

    [out] = call(
        last_kernel,
        where,
        (base, factor, read_queries, *states_got, gated, power, norm_gain.reshape(1, INNER)),
        [shape((CHUNK, INNER), bf16)],
        [
            pltpu.VMEM((HALF, CHUNK, WIDE), f32),
            pltpu.VMEM((CHUNK, INNER), bf16),
            dma((PARTS,)),
        ],
        "last",
        out_specs=[anywhere],
    )
    return out


def solution(mesh):
    ctx, head = mesh.devices.shape
    split = Mesh(mesh.devices.reshape(ctx, head // CORES, CORES), ("ctx", "z", "core"))
    tokens = P(("ctx", "z", "core"), None)
    return jax.shard_map(
        local,
        mesh=split,
        in_specs=(tokens,) * 5 + (P(("z", "core")),) * 3 + (P(), P("ctx")),
        out_specs=tokens,
        check_vma=False,
    )
```
